128 devices in a mesh: section: 8 (over y, x_hi), dp: 16 (over z, x_lo, core).
Axes of the slice: x: 4 (x_hi: 2, x_lo: 2; x = x_hi * 2 + x_lo), y: 4, z: 4, core: 2. Of those that a mesh axis runs over, the one named last changes fastest.
Arguments:
- saved: bfloat16 [8, 2048, 7168], P('section', 'dp')
- top_grad: bfloat16 [2048, 7168], P('dp')
- down_weight: bfloat16 [8, 256, 7168], P('section'), may hold values from -0.0625 to 0.0625
- up_weight: bfloat16 [8, 256, 7168], P('section'), may hold values from -0.1875 to 0.1875
Outputs:
- section_grads: bfloat16 [8, 2048, 7168], P('section', 'dp')
- updates: bfloat16 [8, 2, 256, 7168], P('section')
- grad_norms: float32 [8, 2], P('section')
The draws below stay inside these ranges and needn't reach their ends.
All inputs are finite; a program needn't handle non-finite values.
Results may differ from the reference program's by a relative error of at most 0.0087.
Values may be sent and summed in bfloat16 or wider, within the bound.
A program may use at most 128 MiB of HBM per device.

```python
import math
import jax
import jax.numpy as jnp
from jax import lax

D = 7168
LATENT = 256
ITERS = 5
TOKENS = 2048
N_SECTION = 8


def column_scales(width, ratio):
    place = jnp.arange(width, dtype=jnp.float32) / max(width - 1, 1)
    return jnp.exp(place * jnp.log(ratio))


def draw_saved(key, part):
    key = jax.random.fold_in(key, 11)
    shape = (N_SECTION, TOKENS, D)
    base = jnp.clip(jax.random.normal(key, shape, jnp.float32), -6.0, 6.0)
    scales = column_scales(D, 10.0)
    return (base * scales).astype(jnp.bfloat16)


def draw_top_grad(key, part):
    key = jax.random.fold_in(key, 23)
    shape = (TOKENS, D)
    base = jnp.clip(jax.random.normal(key, shape, jnp.float32), -6.0, 6.0)
    scales = column_scales(D, 10.0)
    return (base * scales).astype(jnp.bfloat16)


def shard_levels(own_key, dims, shards, smallest, largest):
    loudness, own = 1.0, jax.random.fold_in(own_key, 6)
    for axis_at, blocks in shards:
        steps = jnp.exp(jax.random.uniform(jax.random.fold_in(own, axis_at), (blocks,), jnp.float32, smallest / len(shards), largest / len(shards)))
        loudness = loudness * jnp.repeat(steps, dims[axis_at] // blocks).reshape([-1 if axis == axis_at else 1 for axis in range(len(dims))])
    return loudness


def centred(stream_key, dims, scale, limit, split=(), kind=jnp.bfloat16):
    values = scale * jax.random.normal(stream_key, dims, jnp.float32)
    if split:
        values = values * shard_levels(stream_key, dims, split, -0.22, 0.18)
    return jnp.clip(values, -limit, limit).astype(kind)


def setup_inputs(seed: int = 0) -> dict:
    streams_of = jax.random.split(jax.random.key(seed), 5)
    saved = draw_saved(jax.random.fold_in(streams_of[4], 71), 0)
    top_grad = draw_top_grad(jax.random.fold_in(streams_of[4], 71), 0)
    down_weight = centred(streams_of[2], (N_SECTION, LATENT, D), D ** -0.5, 0.0625, ((0, 8),))
    up_weight = centred(streams_of[3], (N_SECTION, LATENT, D), (4 * LATENT) ** -0.5, 0.1875, ((0, 8),))
    return {"saved": saved, "top_grad": top_grad, "down_weight": down_weight, "up_weight": up_weight}


def section_backward(section_in, out_grad, w_down, w_up):
    wide_in = section_in.astype(jnp.float32)
    inv_rms = 1.0 / jnp.sqrt(lax.optimization_barrier(jnp.mean(wide_in * wide_in, axis=-1, keepdims=True)) + 1e-06)
    norm_full = wide_in * inv_rms
    normed = norm_full.astype(jnp.bfloat16)
    latent = jnp.dot(normed, w_down.T, preferred_element_type=jnp.float32)
    sigmoid_h = jax.nn.sigmoid(latent)
    act_out = (latent * sigmoid_h).astype(jnp.bfloat16)
    act_grad = jnp.dot(out_grad, w_up.T, preferred_element_type=jnp.float32)
    lat_grad = (act_grad * sigmoid_h * (1.0 + latent * (1.0 - sigmoid_h))).astype(jnp.bfloat16)
    norm_grad = jnp.dot(lat_grad, w_down, preferred_element_type=jnp.float32)
    in_grad = out_grad.astype(jnp.float32) + inv_rms * (norm_grad - norm_full * lax.optimization_barrier(jnp.mean(norm_grad * norm_full, axis=-1, keepdims=True)))
    return (in_grad.astype(jnp.bfloat16), normed, act_out, lat_grad)

def orthogonalize(matrix):
    highest = lax.Precision.HIGHEST
    norm_value = jnp.sqrt(jnp.sum(matrix * matrix))
    ortho = matrix / (norm_value + 1e-07)
    for repeat in range(ITERS):
        gram = jnp.dot(ortho, ortho.T, precision=highest, preferred_element_type=jnp.float32)
        poly = -4.775 * gram + 2.0315 * jnp.dot(gram, gram, precision=highest, preferred_element_type=jnp.float32)
        ortho = 3.4445 * ortho + jnp.dot(poly, ortho, precision=highest, preferred_element_type=jnp.float32)
    return ((0.2 * math.sqrt(D) * ortho).astype(jnp.bfloat16), norm_value)

def reference(saved, top_grad, down_weight, up_weight):
    out_grad = top_grad
    grads_list = [None] * N_SECTION
    update_list = [None] * N_SECTION
    norm_list = [None] * N_SECTION
    for section_no in reversed(range(N_SECTION)):
        in_grad, normed, act_out, lat_grad = section_backward(saved[section_no], out_grad, down_weight[section_no], up_weight[section_no])
        grad_down = jnp.dot(lat_grad.T, normed, preferred_element_type=jnp.float32)
        grad_up = jnp.dot(act_out.T, out_grad, preferred_element_type=jnp.float32)
        upd_down, norm_down = orthogonalize(grad_down)
        upd_up, norm_up = orthogonalize(grad_up)
        update_list[section_no] = jnp.stack([upd_down, upd_up])
        norm_list[section_no] = jnp.stack([norm_down, norm_up])
        grads_list[section_no] = in_grad
        out_grad = in_grad
    return (jnp.stack(grads_list), jnp.stack(update_list), jnp.stack(norm_list))
```

```python
import functools
import math

import jax
import jax.numpy as jnp
from jax import lax
from jax.experimental import pallas as pl
from jax.experimental.pallas import tpu as pltpu
from jax.sharding import PartitionSpec as P

D = 7168
LAT = 256
ITERS = 5
TOK = 128
ROWS = 16
MICROS = TOK // ROWS
CHUNKS = 4
WIDE = D // CHUNKS
BLOCKS = 8
BLOCK = D // BLOCKS
PEERS = 16
SECTIONS = 8

norm_eps = 1e-06
frob_eps = 1e-07
coef_a = 3.4445
coef_b = -4.775
coef_c = 2.0315

MESH = pl.DeviceIdType.MESH
f32 = jnp.float32
bf16 = jnp.bfloat16
HIGHEST = lax.Precision.HIGHEST


def remote(src, dst, send, recv, device):
    return pltpu.make_async_remote_copy(
        src_ref=src, dst_ref=dst, send_sem=send, recv_sem=recv, device_id=device, device_id_type=MESH
    )


def nt_dot(a, b, precision=None):
    return lax.dot_general(
        a, b, (((1,), (1,)), ((), ())), preferred_element_type=f32, precision=precision
    )


def tn_dot(a, b):
    return lax.dot_general(a, b, (((0,), (0,)), ((), ())), preferred_element_type=f32)


def chain_kernel(
    saved, top, w_down, w_up, grads_out, block_out,
    x_v, wd_v, wu_v, wut_v, normed_v, og_v, ig_v, inv_v, latent_v, slope_v, act_v, lat_v,
    big_all, small_all,
    load_sem, chain_send, chain_recv, big_send, big_recv, small_send, small_recv, store_sem,
):
    s = lax.axis_index("section")
    d = lax.axis_index("dp")
    core = lax.rem(d, 2)
    mine = lax.div(d, 2)
    is_top = s == SECTIONS - 1
    has_lower = s > 0

    loads = [
        pltpu.make_async_copy(saved, x_v, load_sem.at[0]),
        pltpu.make_async_copy(w_up, wu_v, load_sem.at[1]),
        pltpu.make_async_copy(w_down, wd_v, load_sem.at[2]),
    ]
    for load in loads:
        load.start()
    top_load = pltpu.make_async_copy(top, og_v, load_sem.at[3])

    @pl.when(is_top)
    def _():
        top_load.start()

    barrier = pltpu.get_barrier_semaphore()
    for k in range(1, PEERS):
        pl.semaphore_signal(
            barrier, inc=1, device_id=(s, lax.rem(d + k, PEERS)), device_id_type=MESH
        )

    @pl.when(jnp.logical_not(is_top))
    def _():
        pl.semaphore_signal(barrier, inc=1, device_id=(s + 1, d), device_id_type=MESH)

    loads[0].wait()

    def norm_rows(m, _):
        rows = pl.ds(pl.multiple_of(m * ROWS, ROWS), ROWS)
        total = jnp.zeros((ROWS, 1), f32)
        for j in range(CHUNKS):
            part = x_v[rows, j * WIDE:(j + 1) * WIDE].astype(f32)
            total += jnp.sum(part * part, axis=1, keepdims=True)
        inv = 1.0 / jnp.sqrt(total * (1.0 / D) + norm_eps)
        inv_v[rows, :] = jnp.broadcast_to(inv, (ROWS, 128))
        for j in range(CHUNKS):
            part = x_v[rows, j * WIDE:(j + 1) * WIDE].astype(f32)
            normed_v[rows, j * WIDE:(j + 1) * WIDE] = (part * inv).astype(bf16)
        return 0

    lax.fori_loop(0, MICROS, norm_rows, 0)
    loads[1].wait()

    def turn(j, _):
        cols = pl.ds(pl.multiple_of(j * LAT, LAT), LAT)
        wut_v[cols, :] = wu_v[:, cols].T
        return 0

    lax.fori_loop(0, D // LAT, turn, 0)
    loads[2].wait()

    def latent_part(j, acc):
        cols = pl.ds(pl.multiple_of(j * BLOCK, BLOCK), BLOCK)
        return acc + nt_dot(normed_v[:, cols], wd_v[:, cols])

    latent = lax.fori_loop(0, BLOCKS, latent_part, jnp.zeros((TOK, LAT), f32))
    sigmoid = 1.0 / (1.0 + jnp.exp(-latent))
    latent_v[...] = latent
    act_v[...] = (latent * sigmoid).astype(bf16)
    slope_v[...] = sigmoid * (1.0 + latent * (1.0 - sigmoid))

    @pl.when(has_lower)
    def _():
        pl.semaphore_wait(barrier, PEERS)

    @pl.when(jnp.logical_not(has_lower))
    def _():
        pl.semaphore_wait(barrier, PEERS - 1)

    def share(src_of, dst, send, recv, target_core, act):
        for k in range(BLOCKS):
            q = lax.rem(mine + k, BLOCKS)
            peer = q * 2 + target_core
            src = src_of(q)
            if k:
                act(remote(src, dst, send, recv, (s, peer)))
            else:
                @pl.when(core != target_core)
                def _():
                    act(remote(src, dst, send, recv, (s, peer)))

    def share_own(src, dst, recv, target_core):
        @pl.when(core == target_core)
        def _():
            pltpu.make_async_copy(src, dst, recv).start()

    def block_cols(q):
        return pl.ds(pl.multiple_of(q * BLOCK, BLOCK), BLOCK)

    def share_normed(act):
        share(lambda q: normed_v.at[:, block_cols(q)], big_all.at[d], big_send, big_recv.at[d], 0, act)
        share(lambda q: act_v, small_all.at[d], small_send, small_recv.at[d], 1, act)

    def start_normed():
        share_normed(lambda copy: copy.start())
        share_own(normed_v.at[:, block_cols(mine)], big_all.at[d], big_recv.at[d], 0)
        share_own(act_v, small_all.at[d], small_recv.at[d], 1)

    early = s < SECTIONS // 2

    @pl.when(early)
    def _():
        start_normed()

    @pl.when(is_top)
    def _():
        top_load.wait()

    def chain_copy(m, j):
        rows = pl.ds(pl.multiple_of(m * ROWS, ROWS), ROWS)
        cols = slice(j * WIDE, (j + 1) * WIDE)
        return remote(
            ig_v.at[rows, cols], og_v.at[rows, cols], chain_send.at[m, j], chain_recv.at[m, j],
            (jnp.maximum(s - 1, 0), d),
        )

    def share_grads(m, act):
        rows = pl.ds(pl.multiple_of(m * ROWS, ROWS), ROWS)
        share(
            lambda q: og_v.at[rows, block_cols(q)], big_all.at[d, rows], big_send, big_recv.at[d], 1, act
        )
        share(lambda q: lat_v.at[rows], small_all.at[d, rows], small_send, small_recv.at[d], 0, act)

    def micro(m, _):
        rows = pl.ds(pl.multiple_of(m * ROWS, ROWS), ROWS)
        acc = jnp.zeros((ROWS, LAT), f32)
        for j in range(CHUNKS):
            cols = slice(j * WIDE, (j + 1) * WIDE)

            @pl.when(jnp.logical_not(is_top))
            def _():
                chain_copy(m, j).wait_recv()

            acc += jnp.dot(og_v[rows, cols], wut_v[cols, :], preferred_element_type=f32)
        lat = (acc * slope_v[rows, :]).astype(bf16)
        lat_v[rows, :] = lat
        inv = inv_v[rows, 0:1]
        mean = jnp.sum(lat.astype(f32) * latent_v[rows, :], axis=1, keepdims=True) * (1.0 / D)
        pull = inv * inv * mean
        for j in range(CHUNKS):
            cols = slice(j * WIDE, (j + 1) * WIDE)
            ng = jnp.dot(lat, wd_v[:, cols], preferred_element_type=f32)
            out = og_v[rows, cols].astype(f32) + inv * ng - pull * x_v[rows, cols].astype(f32)
            ig_v[rows, cols] = out.astype(bf16)

            @pl.when(has_lower)
            def _():
                chain_copy(m, j).start()

        share_grads(m, lambda copy: copy.start())
        share_own(og_v.at[rows, block_cols(mine)], big_all.at[d, rows], big_recv.at[d], 1)
        share_own(lat_v.at[rows], small_all.at[d, rows], small_recv.at[d], 0)
        return 0

    lax.fori_loop(0, MICROS, micro, 0)

    @pl.when(jnp.logical_not(early))
    def _():
        start_normed()

    store = pltpu.make_async_copy(ig_v, grads_out, store_sem)
    store.start()

    def arrived(p, _):
        pltpu.make_async_copy(big_all.at[p], big_all.at[p], big_recv.at[p]).wait()
        pltpu.make_async_copy(small_all.at[p], small_all.at[p], small_recv.at[p]).wait()
        return 0

    lax.fori_loop(0, PEERS, arrived, 0)

    left = small_all[...].reshape(PEERS * TOK, LAT)
    block_out[...] = tn_dot(left, big_all[...].reshape(PEERS * TOK, BLOCK)).astype(bf16)

    share_normed(lambda copy: copy.wait_send())

    def sent(m, _):
        share_grads(m, lambda copy: copy.wait_send())

        @pl.when(has_lower)
        def _():
            for j in range(CHUNKS):
                chain_copy(m, j).wait_send()

        return 0

    lax.fori_loop(0, MICROS, sent, 0)
    store.wait()


def chain(saved, top, w_down, w_up):
    hbm = pl.BlockSpec(memory_space=pl.ANY)
    vmem = pl.BlockSpec(memory_space=pltpu.VMEM)
    dma = pltpu.SemaphoreType.DMA
    return pl.pallas_call(
        chain_kernel,
        out_shape=(
            jax.ShapeDtypeStruct((TOK, D), bf16),
            jax.ShapeDtypeStruct((LAT, BLOCK), bf16),
        ),
        in_specs=[hbm] * 4,
        out_specs=(hbm, vmem),
        scratch_shapes=[
            pltpu.VMEM((TOK, D), bf16),
            pltpu.VMEM((LAT, D), bf16),
            pltpu.VMEM((LAT, D), bf16),
            pltpu.VMEM((D, LAT), bf16),
            pltpu.VMEM((TOK, D), bf16),
            pltpu.VMEM((TOK, D), bf16),
            pltpu.VMEM((TOK, D), bf16),
            pltpu.VMEM((TOK, 128), f32),
            pltpu.VMEM((TOK, LAT), f32),
            pltpu.VMEM((TOK, LAT), f32),
            pltpu.VMEM((TOK, LAT), bf16),
            pltpu.VMEM((TOK, LAT), bf16),
            pltpu.VMEM((PEERS, TOK, BLOCK), bf16),
            pltpu.VMEM((PEERS, TOK, LAT), bf16),
            dma((4,)),
            dma((MICROS, CHUNKS)),
            dma((MICROS, CHUNKS)),
            dma(()),
            dma((PEERS,)),
            dma(()),
            dma((PEERS,)),
            dma(()),
        ],
        name="chain",
        compiler_params=pltpu.CompilerParams(
            collective_id=0, has_side_effects=True, vmem_limit_bytes=56 * 2**20
        ),
    )(saved, top, w_down, w_up)


HALF = LAT // 2


def newton_schulz(gram):
    total = None
    for step in range(ITERS):
        square = jnp.dot(gram, gram, precision=HIGHEST, preferred_element_type=f32)
        eye = (
            lax.broadcasted_iota(jnp.int32, (LAT, LAT), 0)
            == lax.broadcasted_iota(jnp.int32, (LAT, LAT), 1)
        ).astype(f32)
        poly = coef_a * eye + coef_b * gram + coef_c * square
        if total is None:
            total = poly
        else:
            total = jnp.dot(poly, total, precision=HIGHEST, preferred_element_type=f32)
        if step < ITERS - 1:
            half = jnp.dot(poly, gram, precision=HIGHEST, preferred_element_type=f32)
            gram = jnp.dot(half, poly, precision=HIGHEST, preferred_element_type=f32)
    return total


def gather_kernel(
    block, gathered, poly_out, norm_out,
    own, other, poly_v, norm_v,
    send, recv, core_send, core_recv, small_send, small_recv, store_sem,
):
    s = lax.axis_index("section")
    d = lax.axis_index("dp")
    core = lax.rem(d, 2)
    q = lax.div(d, 2)
    x = lax.rem(q, 2)
    z = lax.div(q, 2)
    up = lax.rem(z + 1, 4)
    down = lax.rem(z + 3, 4)
    far = lax.rem(z + 2, 4)

    def device(z_at, x_at):
        return (s, z_at * 4 + x_at * 2 + core)

    across = device(z, 1 - x)
    above = device(up, x)
    below = device(down, x)
    sibling = (s, q * 2 + 1 - core)

    barrier = pltpu.get_barrier_semaphore()
    for neighbour in (across, above, below, sibling):
        pl.semaphore_signal(barrier, inc=1, device_id=neighbour, device_id_type=MESH)
    own[q] = block[...]
    pl.semaphore_wait(barrier, 4)

    copies = []

    def at(z_at, x_at, half):
        return own.at[z_at * 2 + x_at, pl.ds(half * HALF, HALF)]

    def forward(z_at, x_at, half, to, lane):
        copy = remote(
            at(z_at, x_at, half), at(z_at, x_at, half),
            send.at[len(copies)], recv.at[z_at * 2 + x_at, half], to,
        )
        copy.start()
        copies.append(copy)

    def wait(z_at, x_at, half):
        part = at(z_at, x_at, half)
        pltpu.make_async_copy(part, part, recv.at[z_at * 2 + x_at, half]).wait()

    def to_sibling(z_at, x_at, half):
        n = z_at * 2 + x_at
        copy = remote(
            own.at[n, pl.ds(half * HALF, HALF)], other.at[n, pl.ds(half * HALF, HALF)],
            core_send, core_recv, sibling,
        )
        copy.start()
        return copy

    core_copies = []
    gram = jnp.zeros((LAT, LAT), f32)

    def used(z_at, x_at):
        part = own[z_at * 2 + x_at]
        return nt_dot(part, part)

    for half in (0, 1):
        forward(z, x, half, above, 0)
        forward(z, x, half, below, 1)
        forward(z, x, half, across, 2)
    for half in (0, 1):
        core_copies.append(to_sibling(z, x, half))
    gram += used(z, x)

    wait(down, x, 0)
    forward(down, x, 0, above, 0)
    core_copies.append(to_sibling(down, x, 0))
    wait(up, x, 0)
    core_copies.append(to_sibling(up, x, 0))
    wait(z, 1 - x, 0)
    forward(z, 1 - x, 0, above, 0)
    forward(z, 1 - x, 0, below, 1)
    core_copies.append(to_sibling(z, 1 - x, 0))
    wait(up, x, 1)
    forward(up, x, 1, below, 1)
    core_copies.append(to_sibling(up, x, 1))
    wait(down, x, 1)
    core_copies.append(to_sibling(down, x, 1))
    wait(z, 1 - x, 1)
    forward(z, 1 - x, 1, above, 0)
    forward(z, 1 - x, 1, below, 1)
    core_copies.append(to_sibling(z, 1 - x, 1))
    gram += used(down, x)
    gram += used(up, x)
    gram += used(z, 1 - x)
    for half in (0, 1):
        wait(far, x, half)
        forward(far, x, half, across, 2)
        core_copies.append(to_sibling(far, x, half))
    gram += used(far, x)
    for z_at in (up, down):
        for half in (0, 1):
            wait(z_at, 1 - x, half)
            core_copies.append(to_sibling(z_at, 1 - x, half))
        gram += used(z_at, 1 - x)
    for half in (0, 1):
        wait(far, 1 - x, half)
        core_copies.append(to_sibling(far, 1 - x, half))
    gram += used(far, 1 - x)
    store_own = pltpu.make_async_copy(own, gathered.at[core], store_sem.at[0])
    store_own.start()

    diagonal = (
        lax.broadcasted_iota(jnp.int32, (LAT, LAT), 0)
        == lax.broadcasted_iota(jnp.int32, (LAT, LAT), 1)
    )
    total = jnp.sum(
        jnp.sum(jnp.where(diagonal, gram, 0.0), axis=1, keepdims=True), axis=0, keepdims=True
    )
    norm = jnp.sqrt(total)
    scale = 1.0 / (norm + frob_eps)
    poly = newton_schulz(gram * scale * scale) * (scale * (0.2 * math.sqrt(D)))
    high = poly.astype(bf16)
    poly_v[core, 0] = high
    poly_v[core, 1] = (poly - high.astype(f32)).astype(bf16)
    norm_v[core] = jnp.broadcast_to(norm, (8, 128))
    give = [
        remote(poly_v.at[core], poly_v.at[core], small_send.at[0], small_recv.at[0], sibling),
        remote(norm_v.at[core], norm_v.at[core], small_send.at[1], small_recv.at[1], sibling),
    ]
    for copy in give:
        copy.start()

    pltpu.make_async_copy(other, other, core_recv).wait()
    store_other = pltpu.make_async_copy(other, gathered.at[1 - core], store_sem.at[1])
    store_other.start()
    theirs = 1 - core
    pltpu.make_async_copy(poly_v.at[theirs], poly_v.at[theirs], small_recv.at[0]).wait()
    pltpu.make_async_copy(norm_v.at[theirs], norm_v.at[theirs], small_recv.at[1]).wait()
    poly_out[...] = poly_v[...]
    norm_out[...] = norm_v[...]
    for copy in copies + core_copies + give:
        copy.wait_send()
    store_own.wait()
    store_other.wait()


def gather(block):
    hbm = pl.BlockSpec(memory_space=pl.ANY)
    vmem = pl.BlockSpec(memory_space=pltpu.VMEM)
    dma = pltpu.SemaphoreType.DMA
    return pl.pallas_call(
        gather_kernel,
        out_shape=(
            jax.ShapeDtypeStruct((2, BLOCKS, LAT, BLOCK), bf16),
            jax.ShapeDtypeStruct((2, 2, LAT, LAT), bf16),
            jax.ShapeDtypeStruct((2, 8, 128), f32),
        ),
        in_specs=[vmem],
        out_specs=(hbm, vmem, vmem),
        scratch_shapes=[
            pltpu.VMEM((BLOCKS, LAT, BLOCK), bf16),
            pltpu.VMEM((BLOCKS, LAT, BLOCK), bf16),
            pltpu.VMEM((2, 2, LAT, LAT), bf16),
            pltpu.VMEM((2, 8, 128), f32),
            dma((14,)),
            dma((BLOCKS, 2)),
            dma(()),
            dma(()),
            dma((2,)),
            dma((2,)),
            dma((2,)),
        ],
        name="gather",
        compiler_params=pltpu.CompilerParams(
            collective_id=1, has_side_effects=True, vmem_limit_bytes=48 * 2**20
        ),
    )(block)


def update_kernel(poly, block, out):
    both = poly[0].reshape(2 * LAT, LAT)
    product = jnp.dot(both, block[0, 0], preferred_element_type=f32)
    out[0, 0] = (product[:LAT] + product[LAT:]).astype(bf16)


def update(poly, gathered):
    return pl.pallas_call(
        update_kernel,
        grid=(2, BLOCKS),
        out_shape=jax.ShapeDtypeStruct((1, 2, LAT, D), bf16),
        in_specs=[
            pl.BlockSpec((1, 2, LAT, LAT), lambda i, j: (i, 0, 0, 0)),
            pl.BlockSpec((1, 1, LAT, BLOCK), lambda i, j: (i, j, 0, 0)),
        ],
        out_specs=pl.BlockSpec((1, 1, LAT, BLOCK), lambda i, j: (0, i, 0, j)),
        name="update",
    )(poly, gathered)


def per_device(saved, top_grad, down_weight, up_weight):
    grads, block = chain(saved[0], top_grad, down_weight[0], up_weight[0])
    gathered, poly, norms = gather(block)
    return grads[None], update(poly, gathered), norms[:, 0, 0][None]


def solution(mesh):
    return jax.shard_map(
        per_device,
        mesh=mesh,
        in_specs=(
            P("section", "dp", None),
            P("dp", None),
            P("section", None, None),
            P("section", None, None),
        ),
        out_specs=(P("section", "dp", None), P("section", None, None, None), P("section", None)),
        check_vma=False,
    )
```

```python
import functools
import math

import jax
import jax.numpy as jnp
from jax import lax
from jax.experimental import pallas as pl
from jax.experimental.pallas import tpu as pltpu
from jax.sharding import PartitionSpec as P

D = 7168
LAT = 256
ITERS = 5
TOK = 128
ROWS = 16
MICROS = TOK // ROWS
CHUNKS = 4
WIDE = D // CHUNKS
HALF = LAT // 2
BLOCKS = 8
BLOCK = D // BLOCKS
PEERS = 8
Z = 4
SPAN = D // Z
SECTIONS = 8

norm_eps = 1e-06
frob_eps = 1e-07
coef_a = 3.4445
coef_b = -4.775
coef_c = 2.0315

MESH = pl.DeviceIdType.MESH
f32 = jnp.float32
bf16 = jnp.bfloat16
HIGHEST = lax.Precision.HIGHEST


def remote(src, dst, send, recv, device):
    return pltpu.make_async_remote_copy(
        src_ref=src, dst_ref=dst, send_sem=send, recv_sem=recv, device_id=device, device_id_type=MESH
    )


def nt_dot(a, b, precision=None):
    return lax.dot_general(
        a, b, (((1,), (1,)), ((), ())), preferred_element_type=f32, precision=precision
    )


def tn_dot(a, b):
    return lax.dot_general(a, b, (((0,), (0,)), ((), ())), preferred_element_type=f32)


def split(a):
    high = a.astype(bf16)
    return high, (a - high.astype(f32)).astype(bf16)


def dot(a, b):
    return jnp.dot(a, b, preferred_element_type=f32)


def exact_dot(a, b):
    return jnp.dot(a, b, precision=HIGHEST, preferred_element_type=f32)


def three_dot(a, b):
    (a_high, a_low), (b_high, b_low) = split(a), split(b)
    return dot(a_high, b_high) + (dot(a_high, b_low) + dot(a_low, b_high))


def newton_schulz(gram):
    total = None
    eye = diagonal_mask().astype(f32)
    for step in range(ITERS):
        mul = exact_dot if step < 2 else three_dot
        poly = coef_a * eye + coef_b * gram + coef_c * mul(gram, gram)
        if step < ITERS - 1:
            gram = mul(mul(poly, gram), poly)
        total = poly if total is None else three_dot(poly, total)
    return total


def diagonal_mask():
    return lax.broadcasted_iota(jnp.int32, (LAT, LAT), 0) == lax.broadcasted_iota(
        jnp.int32, (LAT, LAT), 1
    )


def backward_kernel(
    saved, top, w_down, w_up, grads_out, gathered, poly_out, norm_out,
    x_v, wd_v, wu_v, wut_v, normed_v, og_v, ig_v, inv_v, latent_v, slope_v, act_v, lat_v,
    big_all, small_all, give_v, take_v, own, poly_v, norm_v,
    load_sem, chain_send, chain_recv, big_send, big_recv, small_send, small_recv, store_sem,
    give_send, give_recv, ring_send, ring_recv, core_send, core_recv, poly_send, poly_recv,
):
    s = lax.axis_index("section")
    d = lax.axis_index("dp")
    core = lax.rem(d, 2)
    q = lax.div(d, 2)
    x = lax.rem(q, 2)
    z = lax.div(q, 2)
    up = lax.rem(z + 1, Z)
    down = lax.rem(z + 3, Z)
    far = lax.rem(z + 2, Z)
    is_top = s == SECTIONS - 1
    has_lower = s > 0

    def device(z_at, x_at, core_at):
        return (s, z_at * 4 + x_at * 2 + core_at)

    across = device(z, 1 - x, core)
    above = device(up, x, core)
    below = device(down, x, core)
    sibling = device(z, x, 1 - core)

    loads = [
        pltpu.make_async_copy(saved, x_v, load_sem.at[0]),
        pltpu.make_async_copy(w_up, wu_v, load_sem.at[1]),
        pltpu.make_async_copy(w_down, wd_v, load_sem.at[2]),
    ]
    for load in loads:
        load.start()
    top_load = pltpu.make_async_copy(top, og_v, load_sem.at[3])

    @pl.when(is_top)
    def _():
        top_load.start()

    barrier = pltpu.get_barrier_semaphore()
    pl.semaphore_signal(barrier, inc=1, device_id=sibling, device_id_type=MESH)
    pl.semaphore_signal(barrier, inc=1, device_id=across, device_id_type=MESH)
    for k in range(1, Z):
        for core_at in range(2):
            pl.semaphore_signal(
                barrier, inc=1, device_id=device(lax.rem(z + k, Z), x, core_at), device_id_type=MESH
            )

    @pl.when(jnp.logical_not(is_top))
    def _():
        pl.semaphore_signal(barrier, inc=1, device_id=(s + 1, d), device_id_type=MESH)

    loads[0].wait()

    def norm_rows(m, _):
        rows = pl.ds(pl.multiple_of(m * ROWS, ROWS), ROWS)
        total = jnp.zeros((ROWS, 1), f32)
        for j in range(CHUNKS):
            part = x_v[rows, j * WIDE:(j + 1) * WIDE].astype(f32)
            total += jnp.sum(part * part, axis=1, keepdims=True)
        inv = 1.0 / jnp.sqrt(total * (1.0 / D) + norm_eps)
        inv_v[rows, :] = jnp.broadcast_to(inv, (ROWS, 128))
        for j in range(CHUNKS):
            part = x_v[rows, j * WIDE:(j + 1) * WIDE].astype(f32)
            normed_v[rows, j * WIDE:(j + 1) * WIDE] = (part * inv).astype(bf16)
        return 0

    lax.fori_loop(0, MICROS, norm_rows, 0)
    loads[1].wait()

    def turn(j, _):
        cols = pl.ds(pl.multiple_of(j * LAT, LAT), LAT)
        wut_v[cols, :] = wu_v[:, cols].T
        return 0

    lax.fori_loop(0, D // LAT, turn, 0)
    loads[2].wait()

    def latent_part(j, acc):
        cols = pl.ds(pl.multiple_of(j * BLOCK, BLOCK), BLOCK)
        return acc + nt_dot(normed_v[:, cols], wd_v[:, cols])

    latent = lax.fori_loop(0, BLOCKS, latent_part, jnp.zeros((TOK, LAT), f32))
    sigmoid = 1.0 / (1.0 + jnp.exp(-latent))
    latent_v[...] = latent
    act_v[...] = (latent * sigmoid).astype(bf16)
    slope_v[...] = sigmoid * (1.0 + latent * (1.0 - sigmoid))

    @pl.when(has_lower)
    def _():
        pl.semaphore_wait(barrier, PEERS + 1)

    @pl.when(jnp.logical_not(has_lower))
    def _():
        pl.semaphore_wait(barrier, PEERS)

    place = z * 2 + core

    def share(src_of, dst, send, recv, target_core, act):
        for k in range(Z):
            z_at = lax.rem(z + k, Z)
            copy = remote(src_of(z_at), dst, send, recv, device(z_at, x, target_core))
            if k:
                act(copy)
            else:
                @pl.when(core != target_core)
                def _():
                    act(copy)

    def share_own(src, dst, recv, target_core):
        @pl.when(core == target_core)
        def _():
            pltpu.make_async_copy(src, dst, recv).start()

    def span(z_at):
        return pl.ds(pl.multiple_of(z_at * SPAN, SPAN), SPAN)

    def share_normed(act):
        share(lambda z_at: normed_v.at[:, span(z_at)], big_all.at[place], big_send, big_recv.at[place], 0, act)
        share(lambda z_at: act_v, small_all.at[place], small_send, small_recv.at[place], 1, act)

    def start_normed():
        share_normed(lambda copy: copy.start())
        share_own(normed_v.at[:, span(z)], big_all.at[place], big_recv.at[place], 0)
        share_own(act_v, small_all.at[place], small_recv.at[place], 1)

    @pl.when(jnp.logical_not(is_top))
    def _():
        start_normed()

    @pl.when(is_top)
    def _():
        top_load.wait()

    def chain_copy(m, j):
        rows = pl.ds(pl.multiple_of(m * ROWS, ROWS), ROWS)
        cols = slice(j * WIDE, (j + 1) * WIDE)
        return remote(
            ig_v.at[rows, cols], og_v.at[rows, cols], chain_send.at[m, j], chain_recv.at[m, j],
            (jnp.maximum(s - 1, 0), d),
        )

    def share_grads(m, act):
        rows = pl.ds(pl.multiple_of(m * ROWS, ROWS), ROWS)
        share(
            lambda z_at: og_v.at[rows, span(z_at)], big_all.at[place, rows], big_send, big_recv.at[place], 1, act
        )
        share(lambda z_at: lat_v.at[rows], small_all.at[place, rows], small_send, small_recv.at[place], 0, act)

    def micro(m, _):
        rows = pl.ds(pl.multiple_of(m * ROWS, ROWS), ROWS)
        acc = jnp.zeros((ROWS, LAT), f32)
        for j in range(CHUNKS):
            cols = slice(j * WIDE, (j + 1) * WIDE)

            @pl.when(jnp.logical_not(is_top))
            def _():
                chain_copy(m, j).wait_recv()

            acc += dot(og_v[rows, cols], wut_v[cols, :])
        lat = (acc * slope_v[rows, :]).astype(bf16)
        lat_v[rows, :] = lat
        inv = inv_v[rows, 0:1]
        mean = jnp.sum(lat.astype(f32) * latent_v[rows, :], axis=1, keepdims=True) * (1.0 / D)
        pull = inv * inv * mean
        for j in range(CHUNKS):
            cols = slice(j * WIDE, (j + 1) * WIDE)
            ng = dot(lat, wd_v[:, cols])
            out = og_v[rows, cols].astype(f32) + inv * ng - pull * x_v[rows, cols].astype(f32)
            ig_v[rows, cols] = out.astype(bf16)

            @pl.when(has_lower)
            def _():
                chain_copy(m, j).start()

        share_grads(m, lambda copy: copy.start())
        share_own(og_v.at[rows, span(z)], big_all.at[place, rows], big_recv.at[place], 1)
        share_own(lat_v.at[rows], small_all.at[place, rows], small_recv.at[place], 0)
        return 0

    lax.fori_loop(0, MICROS, micro, 0)

    @pl.when(is_top)
    def _():
        start_normed()

    store = pltpu.make_async_copy(ig_v, grads_out, store_sem.at[0])
    store.start()

    def arrived(p, _):
        pltpu.make_async_copy(big_all.at[p], big_all.at[p], big_recv.at[p]).wait()
        pltpu.make_async_copy(small_all.at[p], small_all.at[p], small_recv.at[p]).wait()
        return 0

    lax.fori_loop(0, PEERS, arrived, 0)

    left = small_all[...].reshape(PEERS * TOK, LAT).T

    def half_cols(x_at):
        return pl.ds(pl.multiple_of(x_at * BLOCK, BLOCK), BLOCK)

    def half_rows(half):
        return pl.ds(half * HALF, HALF)

    right = big_all[:, :, half_cols(1 - x)].reshape(PEERS * TOK, BLOCK)
    gives = []
    for half in range(2):
        give_v[half_rows(half)] = dot(left[half * HALF:(half + 1) * HALF], right).astype(bf16)
        copy = remote(
            give_v.at[half_rows(half)], take_v.at[half_rows(half)], give_send.at[half], give_recv.at[half], across
        )
        copy.start()
        gives.append(copy)
    mine = dot(left, big_all[:, :, half_cols(x)].reshape(PEERS * TOK, BLOCK))

    ring_copies = []
    core_copies = []

    def at(z_at, x_at, half):
        return own.at[z_at * 2 + x_at, half_rows(half)]

    def forward(z_at, x_at, half, to):
        copy = remote(
            at(z_at, x_at, half), at(z_at, x_at, half),
            ring_send.at[len(ring_copies)], ring_recv.at[z_at * 2 + x_at, half], to,
        )
        copy.start()
        ring_copies.append(copy)

    def to_sibling(z_at, x_at, half):
        copy = remote(
            at(z_at, x_at, half), gathered.at[core, z_at * 2 + x_at, half_rows(half)], core_send, core_recv, sibling
        )
        copy.start()
        core_copies.append(copy)

    def wait(z_at, x_at, half):
        part = at(z_at, x_at, half)
        pltpu.make_async_copy(part, part, ring_recv.at[z_at * 2 + x_at, half]).wait()

    def used(z_at, x_at):
        part = own[z_at * 2 + x_at]
        return nt_dot(part, part)

    for half in range(2):
        gives[half].wait_recv()
        total = mine[half * HALF:(half + 1) * HALF] + take_v[half_rows(half)].astype(f32)
        own[q, half_rows(half)] = total.astype(bf16)
        forward(z, x, half, above)
        forward(z, x, half, below)
        forward(z, x, half, across)
        to_sibling(z, x, half)
    gram = used(z, x)

    wait(down, x, 0)
    forward(down, x, 0, above)
    to_sibling(down, x, 0)
    wait(up, x, 0)
    to_sibling(up, x, 0)
    wait(z, 1 - x, 0)
    forward(z, 1 - x, 0, above)
    forward(z, 1 - x, 0, below)
    to_sibling(z, 1 - x, 0)
    wait(up, x, 1)
    forward(up, x, 1, below)
    to_sibling(up, x, 1)
    wait(down, x, 1)
    to_sibling(down, x, 1)
    wait(z, 1 - x, 1)
    forward(z, 1 - x, 1, above)
    forward(z, 1 - x, 1, below)
    to_sibling(z, 1 - x, 1)
    gram += used(down, x)
    gram += used(up, x)
    gram += used(z, 1 - x)
    for half in range(2):
        wait(far, x, half)
        forward(far, x, half, across)
        to_sibling(far, x, half)
    gram += used(far, x)
    for z_at in (up, down):
        for half in range(2):
            wait(z_at, 1 - x, half)
            to_sibling(z_at, 1 - x, half)
        gram += used(z_at, 1 - x)
    for half in range(2):
        wait(far, 1 - x, half)
        to_sibling(far, 1 - x, half)
    gram += used(far, 1 - x)
    store_own = pltpu.make_async_copy(own, gathered.at[core], store_sem.at[1])
    store_own.start()

    squares = jnp.where(diagonal_mask(), gram, 0.0)
    norm = jnp.sqrt(jnp.sum(jnp.sum(squares, axis=1, keepdims=True), axis=0, keepdims=True))
    scale = 1.0 / (norm + frob_eps)
    poly = newton_schulz(gram * scale * scale) * (scale * (0.2 * math.sqrt(D)))
    high, low = split(poly)
    poly_v[core, 0] = high
    poly_v[core, 1] = low
    norm_v[core] = jnp.broadcast_to(norm, (8, 128))
    polys = [
        remote(poly_v.at[core], poly_v.at[core], poly_send.at[0], poly_recv.at[0], sibling),
        remote(norm_v.at[core], norm_v.at[core], poly_send.at[1], poly_recv.at[1], sibling),
    ]
    for copy in polys:
        copy.start()

    theirs = 1 - core
    pltpu.make_async_copy(gathered.at[theirs], gathered.at[theirs], core_recv).wait()
    pltpu.make_async_copy(poly_v.at[theirs], poly_v.at[theirs], poly_recv.at[0]).wait()
    pltpu.make_async_copy(norm_v.at[theirs], norm_v.at[theirs], poly_recv.at[1]).wait()
    poly_out[...] = poly_v[...]
    norm_out[...] = norm_v[...]

    share_normed(lambda copy: copy.wait_send())

    def sent(m, _):
        share_grads(m, lambda copy: copy.wait_send())

        @pl.when(has_lower)
        def _():
            for j in range(CHUNKS):
                chain_copy(m, j).wait_send()

        return 0

    lax.fori_loop(0, MICROS, sent, 0)
    for copy in gives + ring_copies + core_copies + polys:
        copy.wait_send()
    store.wait()
    store_own.wait()


def backward(saved, top, w_down, w_up):
    hbm = pl.BlockSpec(memory_space=pl.ANY)
    vmem = pl.BlockSpec(memory_space=pltpu.VMEM)
    dma = pltpu.SemaphoreType.DMA
    return pl.pallas_call(
        backward_kernel,
        out_shape=(
            pltpu.VMEM((TOK, D), bf16),
            pltpu.VMEM((2, BLOCKS, LAT, BLOCK), bf16),
            pltpu.VMEM((2, 2, LAT, LAT), bf16),
            pltpu.VMEM((2, 8, 128), f32),
        ),
        in_specs=[hbm] * 4,
        out_specs=(hbm, hbm, vmem, vmem),
        scratch_shapes=[
            pltpu.VMEM((TOK, D), bf16),
            pltpu.VMEM((LAT, D), bf16),
            pltpu.VMEM((LAT, D), bf16),
            pltpu.VMEM((D, LAT), bf16),
            pltpu.VMEM((TOK, D), bf16),
            pltpu.VMEM((TOK, D), bf16),
            pltpu.VMEM((TOK, D), bf16),
            pltpu.VMEM((TOK, 128), f32),
            pltpu.VMEM((TOK, LAT), f32),
            pltpu.VMEM((TOK, LAT), f32),
            pltpu.VMEM((TOK, LAT), bf16),
            pltpu.VMEM((TOK, LAT), bf16),
            pltpu.VMEM((PEERS, TOK, SPAN), bf16),
            pltpu.VMEM((PEERS, TOK, LAT), bf16),
            pltpu.VMEM((LAT, BLOCK), bf16),
            pltpu.VMEM((LAT, BLOCK), bf16),
            pltpu.VMEM((BLOCKS, LAT, BLOCK), bf16),
            pltpu.VMEM((2, 2, LAT, LAT), bf16),
            pltpu.VMEM((2, 8, 128), f32),
            dma((4,)),
            dma((MICROS, CHUNKS)),
            dma((MICROS, CHUNKS)),
            dma(()),
            dma((PEERS,)),
            dma(()),
            dma((PEERS,)),
            dma((2,)),
            dma((2,)),
            dma((2,)),
            dma((14,)),
            dma((BLOCKS, 2)),
            dma(()),
            dma(()),
            dma((2,)),
            dma((2,)),
        ],
        name="backward",
        compiler_params=pltpu.CompilerParams(
            collective_id=0, has_side_effects=True, vmem_limit_bytes=40 * 2**20
        ),
    )(saved, top, w_down, w_up)


def update_kernel(poly, block, norms, grads, out, norm_out, grads_out, stage, store_sem):
    stores = [pltpu.make_async_copy(grads, grads_out, store_sem.at[2 * BLOCKS])]
    stores[0].start()
    column = lax.broadcasted_iota(jnp.int32, (1, 2), 1)
    norm_out[...] = jnp.where(column == 0, norms[0, 0:1, 0:1], norms[1, 0:1, 0:1])
    for i in range(2):
        for j in range(BLOCKS):
            right = block[i, j]
            stage[i, j] = (dot(poly[i, 0], right) + dot(poly[i, 1], right)).astype(bf16)
            store = pltpu.make_async_copy(
                stage.at[i, j], out.at[0, i, :, pl.ds(j * BLOCK, BLOCK)], store_sem.at[i * BLOCKS + j]
            )
            store.start()
            stores.append(store)
    for store in stores:
        store.wait()


def update(poly, gathered, norms, grads):
    hbm = pl.BlockSpec(memory_space=pl.ANY)
    vmem = pl.BlockSpec(memory_space=pltpu.VMEM)
    return pl.pallas_call(
        update_kernel,
        out_shape=(
            jax.ShapeDtypeStruct((1, 2, LAT, D), bf16),
            jax.ShapeDtypeStruct((1, 2), f32),
            jax.ShapeDtypeStruct((TOK, D), bf16),
        ),
        in_specs=[vmem] * 4,
        out_specs=(hbm, vmem, hbm),
        scratch_shapes=[
            pltpu.VMEM((2, BLOCKS, LAT, BLOCK), bf16),
            pltpu.SemaphoreType.DMA((2 * BLOCKS + 1,)),
        ],
        name="update",
        compiler_params=pltpu.CompilerParams(vmem_limit_bytes=30 * 2**20),
    )(*[pltpu.with_memory_space_constraint(a, pltpu.VMEM) for a in (poly, gathered, norms, grads)])


def per_device(saved, top_grad, down_weight, up_weight):
    grads, gathered, poly, norms = backward(
        *[pltpu.with_memory_space_constraint(a, pltpu.HBM) for a in (saved[0], top_grad, down_weight[0], up_weight[0])]
    )
    updates, norm_values, grads = update(poly, gathered, norms, grads)
    return grads[None], updates, norm_values


def solution(mesh):
    return jax.shard_map(
        per_device,
        mesh=mesh,
        in_specs=(
            P("section", "dp", None),
            P("dp", None),
            P("section", None, None),
            P("section", None, None),
        ),
        out_specs=(P("section", "dp", None), P("section", None, None, None), P("section", None)),
        check_vma=False,
    )
```

```python
import functools
import math

import jax
import jax.numpy as jnp
from jax import lax
from jax.experimental import pallas as pl
from jax.experimental.pallas import tpu as pltpu
from jax.sharding import PartitionSpec as P

D = 7168
LAT = 256
ITERS = 5
TOK = 128
ROWS = 16
PAIRS = TOK // ROWS
CHUNKS = 4
WIDE = D // CHUNKS
SMALL = 8
SMALLS = TOK // SMALL
PACK = D // 2
PARTS = ((0, 1024), (1024, 1024), (2048, 1024), (3072, 512))
HALF = LAT // 2
BLOCKS = 8
BLOCK = D // BLOCKS
PEERS = 8
Z = 4
SPAN = D // Z
SECTIONS = 8

norm_eps = 1e-06
frob_eps = 1e-07
coef_a = 3.4445
coef_b = -4.775
coef_c = 2.0315

MESH = pl.DeviceIdType.MESH
f32 = jnp.float32
bf16 = jnp.bfloat16
HIGHEST = lax.Precision.HIGHEST


def remote(src, dst, send, recv, device):
    return pltpu.make_async_remote_copy(
        src_ref=src, dst_ref=dst, send_sem=send, recv_sem=recv, device_id=device, device_id_type=MESH
    )


def nt_dot(a, b, precision=None):
    return lax.dot_general(
        a, b, (((1,), (1,)), ((), ())), preferred_element_type=f32, precision=precision
    )


def tn_dot(a, b):
    return lax.dot_general(a, b, (((0,), (0,)), ((), ())), preferred_element_type=f32)


def split(a):
    high = a.astype(bf16)
    return high, (a - high.astype(f32)).astype(bf16)


def dot(a, b):
    return jnp.dot(a, b, preferred_element_type=f32)


def exact_dot(a, b):
    return jnp.dot(a, b, precision=HIGHEST, preferred_element_type=f32)


def three_dot(a, b):
    (a_high, a_low), (b_high, b_low) = split(a), split(b)
    return dot(a_high, b_high) + (dot(a_high, b_low) + dot(a_low, b_high))


def newton_schulz(gram):
    total = None
    eye = diagonal_mask().astype(f32)
    for step in range(ITERS):
        mul = exact_dot if step < 2 else three_dot
        poly = coef_a * eye + coef_b * gram + coef_c * mul(gram, gram)
        if step < ITERS - 1:
            gram = mul(mul(poly, gram), poly)
        total = poly if total is None else three_dot(poly, total)
    return total


def diagonal_mask():
    return lax.broadcasted_iota(jnp.int32, (LAT, LAT), 0) == lax.broadcasted_iota(
        jnp.int32, (LAT, LAT), 1
    )


def backward_kernel(
    saved, top, w_down, w_up, grads_out, gathered, poly_out, norm_out,
    x_v, x_p, wd_v, wu_v, wut_v, normed_v, og_v, og_p, ig_v, ig_p, inv_v, latent_v, slope_v, act_v, lat_v,
    big_all, small_all, give_v, take_v, own, poly_v, norm_v,
    load_sem, wd_sem, chain_send, chain_recv, big_send, big_recv, small_send, small_recv, store_sem,
    give_send, give_recv, ring_send, ring_recv, core_send, core_recv, poly_send, poly_recv,
):
    s = lax.axis_index("section")
    d = lax.axis_index("dp")
    core = lax.rem(d, 2)
    q = lax.div(d, 2)
    x = lax.rem(q, 2)
    z = lax.div(q, 2)
    up = lax.rem(z + 1, Z)
    down = lax.rem(z + 3, Z)
    far = lax.rem(z + 2, Z)
    is_top = s == SECTIONS - 1
    has_lower = s > 0

    def device(z_at, x_at, core_at):
        return (s, z_at * 4 + x_at * 2 + core_at)

    across = device(z, 1 - x, core)
    above = device(up, x, core)
    below = device(down, x, core)
    sibling = device(z, x, 1 - core)

    loads = [
        pltpu.make_async_copy(saved, x_v, load_sem.at[0]),
        pltpu.make_async_copy(w_up, wu_v, load_sem.at[1]),
    ]
    for k in range(BLOCKS):
        part = pl.ds((k % 2) * PACK + (k // 2) * BLOCK, BLOCK)
        loads.append(
            pltpu.make_async_copy(w_down.at[:, pl.ds(k * BLOCK, BLOCK)], wd_v.at[:, part], wd_sem.at[k])
        )
    for load in loads:
        load.start()
    top_load = pltpu.make_async_copy(top, og_v, load_sem.at[2])

    @pl.when(is_top)
    def _():
        top_load.start()

    barrier = pltpu.get_barrier_semaphore()
    pl.semaphore_signal(barrier, inc=1, device_id=sibling, device_id_type=MESH)
    pl.semaphore_signal(barrier, inc=1, device_id=across, device_id_type=MESH)
    for k in range(1, Z):
        for core_at in range(2):
            pl.semaphore_signal(
                barrier, inc=1, device_id=device(lax.rem(z + k, Z), x, core_at), device_id_type=MESH
            )

    @pl.when(jnp.logical_not(is_top))
    def _():
        pl.semaphore_signal(barrier, inc=1, device_id=(s + 1, d), device_id_type=MESH)

    def pack(flat, packed, i):
        rows = pl.ds(pl.multiple_of(i * ROWS, ROWS), ROWS)
        for k in range(Z):
            even = flat[rows, 2 * k * BLOCK:(2 * k + 1) * BLOCK].astype(f32)
            odd = flat[rows, (2 * k + 1) * BLOCK:(2 * k + 2) * BLOCK].astype(f32)
            cols = slice(k * BLOCK, (k + 1) * BLOCK)
            packed[2 * i, :, cols] = jnp.concatenate([even[:SMALL], odd[:SMALL]], axis=0).astype(bf16)
            packed[2 * i + 1, :, cols] = jnp.concatenate([even[SMALL:], odd[SMALL:]], axis=0).astype(bf16)

    def unpack(packed, flat, i):
        rows = pl.ds(pl.multiple_of(i * ROWS, ROWS), ROWS)
        for k in range(Z):
            cols = slice(k * BLOCK, (k + 1) * BLOCK)
            first = packed[2 * i, :, cols].astype(f32)
            second = packed[2 * i + 1, :, cols].astype(f32)
            even = jnp.concatenate([first[:SMALL], second[:SMALL]], axis=0)
            odd = jnp.concatenate([first[SMALL:], second[SMALL:]], axis=0)
            flat[rows, 2 * k * BLOCK:(2 * k + 1) * BLOCK] = even.astype(bf16)
            flat[rows, (2 * k + 1) * BLOCK:(2 * k + 2) * BLOCK] = odd.astype(bf16)

    loads[0].wait()

    def norm_rows(m, _):
        rows = pl.ds(pl.multiple_of(m * ROWS, ROWS), ROWS)
        total = jnp.zeros((ROWS, 1), f32)
        for j in range(CHUNKS):
            part = x_v[rows, j * WIDE:(j + 1) * WIDE].astype(f32)
            total += jnp.sum(part * part, axis=1, keepdims=True)
        inv = 1.0 / jnp.sqrt(total * (1.0 / D) + norm_eps)
        inv_v[rows, :] = jnp.broadcast_to(inv, (ROWS, 128))
        for j in range(CHUNKS):
            part = x_v[rows, j * WIDE:(j + 1) * WIDE].astype(f32)
            normed_v[rows, j * WIDE:(j + 1) * WIDE] = (part * inv).astype(bf16)
        pack(x_v, x_p, m)
        return 0

    lax.fori_loop(0, PAIRS, norm_rows, 0)
    loads[1].wait()

    def turn(k, _):
        for odd in range(2):
            cols = pl.ds(pl.multiple_of((2 * k + odd) * BLOCK, BLOCK), BLOCK)
            rows = pl.ds(pl.multiple_of(k * BLOCK, BLOCK), BLOCK)
            wut_v[rows, odd * LAT:(odd + 1) * LAT] = wu_v[:, cols].T
        return 0

    lax.fori_loop(0, Z, turn, 0)
    for load in loads[2:]:
        load.wait()

    def latent_part(k, acc):
        for odd in range(2):
            cols = pl.ds(pl.multiple_of((2 * k + odd) * BLOCK, BLOCK), BLOCK)
            part = pl.ds(pl.multiple_of(odd * PACK + k * BLOCK, BLOCK), BLOCK)
            acc = acc + nt_dot(normed_v[:, cols], wd_v[:, part])
        return acc

    latent = lax.fori_loop(0, Z, latent_part, jnp.zeros((TOK, LAT), f32))
    sigmoid = 1.0 / (1.0 + jnp.exp(-latent))
    latent_v[...] = latent
    act_v[...] = (latent * sigmoid).astype(bf16)
    slope_v[...] = sigmoid * (1.0 + latent * (1.0 - sigmoid))

    @pl.when(has_lower)
    def _():
        pl.semaphore_wait(barrier, PEERS + 1)

    @pl.when(jnp.logical_not(has_lower))
    def _():
        pl.semaphore_wait(barrier, PEERS)

    place = z * 2 + core

    def share(src_of, dst, send, recv, target_core, act):
        for k in range(Z):
            z_at = lax.rem(z + k, Z)
            copy = remote(src_of(z_at), dst, send, recv, device(z_at, x, target_core))
            if k:
                act(copy)
            else:
                @pl.when(core != target_core)
                def _():
                    act(copy)

    def share_own(src, dst, recv, target_core):
        @pl.when(core == target_core)
        def _():
            pltpu.make_async_copy(src, dst, recv).start()

    def span(z_at):
        return pl.ds(pl.multiple_of(z_at * SPAN, SPAN), SPAN)

    def share_normed(act):
        share(lambda z_at: normed_v.at[:, span(z_at)], big_all.at[place], big_send, big_recv.at[place], 0, act)
        share(lambda z_at: act_v, small_all.at[place], small_send, small_recv.at[place], 1, act)

    def start_normed():
        share_normed(lambda copy: copy.start())
        share_own(normed_v.at[:, span(z)], big_all.at[place], big_recv.at[place], 0)
        share_own(act_v, small_all.at[place], small_recv.at[place], 1)

    @pl.when(jnp.logical_not(is_top))
    def _():
        start_normed()

    @pl.when(is_top)
    def _():
        top_load.wait()

        def pack_top(i, _):
            pack(og_v, og_p, i)
            return 0

        lax.fori_loop(0, PAIRS, pack_top, 0)

    def chain_copy(m, j):
        cols = pl.ds(*PARTS[j])
        return remote(
            ig_p.at[m, :, cols], og_p.at[m, :, cols], chain_send.at[m, j], chain_recv.at[m, j],
            (jnp.maximum(s - 1, 0), d),
        )

    def share_grads(m, act):
        rows = pl.ds(pl.multiple_of(m * ROWS, ROWS), ROWS)
        share(
            lambda z_at: og_v.at[rows, span(z_at)], big_all.at[place, rows], big_send, big_recv.at[place], 1, act
        )
        share(lambda z_at: lat_v.at[rows], small_all.at[place, rows], small_send, small_recv.at[place], 0, act)

    def step(m):
        rows = pl.ds(pl.multiple_of(m * SMALL, SMALL), SMALL)
        acc = jnp.zeros((ROWS, 2 * LAT), f32)
        for j, (at, width) in enumerate(PARTS):

            @pl.when(jnp.logical_not(is_top))
            def _():
                chain_copy(m, j).wait_recv()

            acc += dot(og_p[m, :, at:at + width], wut_v[at:at + width, :])
        act_grad = acc[:SMALL, :LAT] + acc[SMALL:, LAT:]
        lat = (act_grad * slope_v[rows, :]).astype(bf16).astype(f32)
        inv = inv_v[rows, 0:1]
        mean = jnp.sum(lat * latent_v[rows, :], axis=1, keepdims=True) * (1.0 / D)
        pull = inv * inv * mean
        lat_twice = jnp.concatenate([lat, lat], axis=0).astype(bf16)
        inv_twice = jnp.concatenate([inv, inv], axis=0)
        pull_twice = jnp.concatenate([pull, pull], axis=0)
        for j, (at, width) in enumerate(PARTS):
            cols = slice(at, at + width)
            even = dot(lat_twice, wd_v[:, at:at + width])
            odd = dot(lat_twice, wd_v[:, PACK + at:PACK + at + width])
            ng = jnp.concatenate([even[:SMALL], odd[SMALL:]], axis=0)
            out = og_p[m, :, cols].astype(f32) + inv_twice * ng - pull_twice * x_p[m, :, cols].astype(f32)
            ig_p[m, :, cols] = out.astype(bf16)

            @pl.when(has_lower)
            def _():
                chain_copy(m, j).start()

        return lat

    def micro(i, _):
        rows = pl.ds(pl.multiple_of(i * ROWS, ROWS), ROWS)
        first = step(2 * i)
        second = step(2 * i + 1)
        lat_v[rows, :] = jnp.concatenate([first, second], axis=0).astype(bf16)

        @pl.when(jnp.logical_not(is_top))
        def _():
            unpack(og_p, og_v, i)

        share_grads(i, lambda copy: copy.start())
        share_own(og_v.at[rows, span(z)], big_all.at[place, rows], big_recv.at[place], 1)
        share_own(lat_v.at[rows], small_all.at[place, rows], small_recv.at[place], 0)
        unpack(ig_p, ig_v, i)
        return 0

    lax.fori_loop(0, PAIRS, micro, 0)

    @pl.when(is_top)
    def _():
        start_normed()

    store = pltpu.make_async_copy(ig_v, grads_out, store_sem.at[0])
    store.start()

    def arrived(p, _):
        pltpu.make_async_copy(big_all.at[p], big_all.at[p], big_recv.at[p]).wait()
        pltpu.make_async_copy(small_all.at[p], small_all.at[p], small_recv.at[p]).wait()
        return 0

    lax.fori_loop(0, PEERS, arrived, 0)

    left = small_all[...].reshape(PEERS * TOK, LAT).T

    def half_cols(x_at):
        return pl.ds(pl.multiple_of(x_at * BLOCK, BLOCK), BLOCK)

    def half_rows(half):
        return pl.ds(half * HALF, HALF)

    right = big_all[:, :, half_cols(1 - x)].reshape(PEERS * TOK, BLOCK)
    gives = []
    for half in range(2):
        give_v[half_rows(half)] = dot(left[half * HALF:(half + 1) * HALF], right).astype(bf16)
        copy = remote(
            give_v.at[half_rows(half)], take_v.at[half_rows(half)], give_send.at[half], give_recv.at[half], across
        )
        copy.start()
        gives.append(copy)
    mine = dot(left, big_all[:, :, half_cols(x)].reshape(PEERS * TOK, BLOCK))

    ring_copies = []
    core_copies = []

    def at(z_at, x_at, half):
        return own.at[z_at * 2 + x_at, half_rows(half)]

    def forward(z_at, x_at, half, to):
        copy = remote(
            at(z_at, x_at, half), at(z_at, x_at, half),
            ring_send.at[len(ring_copies)], ring_recv.at[z_at * 2 + x_at, half], to,
        )
        copy.start()
        ring_copies.append(copy)

    def to_sibling(z_at, x_at, half):
        copy = remote(
            at(z_at, x_at, half), gathered.at[core, z_at * 2 + x_at, half_rows(half)], core_send, core_recv, sibling
        )
        copy.start()
        core_copies.append(copy)

    def wait(z_at, x_at, half):
        part = at(z_at, x_at, half)
        pltpu.make_async_copy(part, part, ring_recv.at[z_at * 2 + x_at, half]).wait()

    def used(z_at, x_at):
        part = own[z_at * 2 + x_at]
        return nt_dot(part, part)

    for half in range(2):
        gives[half].wait_recv()
        total = mine[half * HALF:(half + 1) * HALF] + take_v[half_rows(half)].astype(f32)
        own[q, half_rows(half)] = total.astype(bf16)
        forward(z, x, half, above)
        forward(z, x, half, below)
        forward(z, x, half, across)
        to_sibling(z, x, half)
    gram = used(z, x)

    wait(down, x, 0)
    forward(down, x, 0, above)
    to_sibling(down, x, 0)
    wait(up, x, 0)
    to_sibling(up, x, 0)
    wait(z, 1 - x, 0)
    forward(z, 1 - x, 0, above)
    forward(z, 1 - x, 0, below)
    to_sibling(z, 1 - x, 0)
    wait(up, x, 1)
    forward(up, x, 1, below)
    to_sibling(up, x, 1)
    wait(down, x, 1)
    to_sibling(down, x, 1)
    wait(z, 1 - x, 1)
    forward(z, 1 - x, 1, above)
    forward(z, 1 - x, 1, below)
    to_sibling(z, 1 - x, 1)
    gram += used(down, x)
    gram += used(up, x)
    gram += used(z, 1 - x)
    for half in range(2):
        wait(far, x, half)
        forward(far, x, half, across)
        to_sibling(far, x, half)
    gram += used(far, x)
    for z_at in (up, down):
        for half in range(2):
            wait(z_at, 1 - x, half)
            to_sibling(z_at, 1 - x, half)
        gram += used(z_at, 1 - x)
    for half in range(2):
        wait(far, 1 - x, half)
        to_sibling(far, 1 - x, half)
    gram += used(far, 1 - x)
    store_own = pltpu.make_async_copy(own, gathered.at[core], store_sem.at[1])
    store_own.start()

    squares = jnp.where(diagonal_mask(), gram, 0.0)
    norm = jnp.sqrt(jnp.sum(jnp.sum(squares, axis=1, keepdims=True), axis=0, keepdims=True))
    scale = 1.0 / (norm + frob_eps)
    poly = newton_schulz(gram * scale * scale) * (scale * (0.2 * math.sqrt(D)))
    high, low = split(poly)
    poly_v[core, 0] = high
    poly_v[core, 1] = low
    norm_v[core] = jnp.broadcast_to(norm, (8, 128))
    polys = [
        remote(poly_v.at[core], poly_v.at[core], poly_send.at[0], poly_recv.at[0], sibling),
        remote(norm_v.at[core], norm_v.at[core], poly_send.at[1], poly_recv.at[1], sibling),
    ]
    for copy in polys:
        copy.start()

    theirs = 1 - core
    pltpu.make_async_copy(gathered.at[theirs], gathered.at[theirs], core_recv).wait()
    pltpu.make_async_copy(poly_v.at[theirs], poly_v.at[theirs], poly_recv.at[0]).wait()
    pltpu.make_async_copy(norm_v.at[theirs], norm_v.at[theirs], poly_recv.at[1]).wait()
    poly_out[...] = poly_v[...]
    norm_out[...] = norm_v[...]

    share_normed(lambda copy: copy.wait_send())

    def sent(m, _):
        share_grads(m, lambda copy: copy.wait_send())

        @pl.when(has_lower)
        def _():
            for j in range(len(PARTS)):
                chain_copy(2 * m, j).wait_send()
                chain_copy(2 * m + 1, j).wait_send()

        return 0

    lax.fori_loop(0, PAIRS, sent, 0)
    for copy in gives + ring_copies + core_copies + polys:
        copy.wait_send()
    store.wait()
    store_own.wait()


def backward(saved, top, w_down, w_up):
    hbm = pl.BlockSpec(memory_space=pl.ANY)
    vmem = pl.BlockSpec(memory_space=pltpu.VMEM)
    dma = pltpu.SemaphoreType.DMA
    return pl.pallas_call(
        backward_kernel,
        out_shape=(
            pltpu.VMEM((TOK, D), bf16),
            pltpu.VMEM((2, BLOCKS, LAT, BLOCK), bf16),
            pltpu.VMEM((2, 2, LAT, LAT), bf16),
            pltpu.VMEM((2, 8, 128), f32),
        ),
        in_specs=[hbm] * 4,
        out_specs=(hbm, hbm, vmem, vmem),
        scratch_shapes=[
            pltpu.VMEM((TOK, D), bf16),
            pltpu.VMEM((SMALLS, ROWS, PACK), bf16),
            pltpu.VMEM((LAT, D), bf16),
            pltpu.VMEM((LAT, D), bf16),
            pltpu.VMEM((PACK, 2 * LAT), bf16),
            pltpu.VMEM((TOK, D), bf16),
            pltpu.VMEM((TOK, D), bf16),
            pltpu.VMEM((SMALLS, ROWS, PACK), bf16),
            pltpu.VMEM((TOK, D), bf16),
            pltpu.VMEM((SMALLS, ROWS, PACK), bf16),
            pltpu.VMEM((TOK, 128), f32),
            pltpu.VMEM((TOK, LAT), f32),
            pltpu.VMEM((TOK, LAT), f32),
            pltpu.VMEM((TOK, LAT), bf16),
            pltpu.VMEM((TOK, LAT), bf16),
            pltpu.VMEM((PEERS, TOK, SPAN), bf16),
            pltpu.VMEM((PEERS, TOK, LAT), bf16),
            pltpu.VMEM((LAT, BLOCK), bf16),
            pltpu.VMEM((LAT, BLOCK), bf16),
            pltpu.VMEM((BLOCKS, LAT, BLOCK), bf16),
            pltpu.VMEM((2, 2, LAT, LAT), bf16),
            pltpu.VMEM((2, 8, 128), f32),
            dma((3,)),
            dma((BLOCKS,)),
            dma((SMALLS, len(PARTS))),
            dma((SMALLS, len(PARTS))),
            dma(()),
            dma((PEERS,)),
            dma(()),
            dma((PEERS,)),
            dma((2,)),
            dma((2,)),
            dma((2,)),
            dma((14,)),
            dma((BLOCKS, 2)),
            dma(()),
            dma(()),
            dma((2,)),
            dma((2,)),
        ],
        name="backward",
        compiler_params=pltpu.CompilerParams(
            collective_id=0, has_side_effects=True, vmem_limit_bytes=40 * 2**20
        ),
    )(saved, top, w_down, w_up)


def update_kernel(poly, block, norms, grads, out, norm_out, grads_out, stage, store_sem):
    stores = [pltpu.make_async_copy(grads, grads_out, store_sem.at[2 * BLOCKS])]
    stores[0].start()
    column = lax.broadcasted_iota(jnp.int32, (1, 2), 1)
    norm_out[...] = jnp.where(column == 0, norms[0, 0:1, 0:1], norms[1, 0:1, 0:1])
    for i in range(2):
        for j in range(BLOCKS):
            right = block[i, j]
            stage[i, j] = (dot(poly[i, 0], right) + dot(poly[i, 1], right)).astype(bf16)
            store = pltpu.make_async_copy(
                stage.at[i, j], out.at[0, i, :, pl.ds(j * BLOCK, BLOCK)], store_sem.at[i * BLOCKS + j]
            )
            store.start()
            stores.append(store)
    for store in stores:
        store.wait()


def update(poly, gathered, norms, grads):
    hbm = pl.BlockSpec(memory_space=pl.ANY)
    vmem = pl.BlockSpec(memory_space=pltpu.VMEM)
    return pl.pallas_call(
        update_kernel,
        out_shape=(
            jax.ShapeDtypeStruct((1, 2, LAT, D), bf16),
            jax.ShapeDtypeStruct((1, 2), f32),
            jax.ShapeDtypeStruct((TOK, D), bf16),
        ),
        in_specs=[vmem] * 4,
        out_specs=(hbm, vmem, hbm),
        scratch_shapes=[
            pltpu.VMEM((2, BLOCKS, LAT, BLOCK), bf16),
            pltpu.SemaphoreType.DMA((2 * BLOCKS + 1,)),
        ],
        name="update",
        compiler_params=pltpu.CompilerParams(vmem_limit_bytes=30 * 2**20),
    )(*[pltpu.with_memory_space_constraint(a, pltpu.VMEM) for a in (poly, gathered, norms, grads)])


def per_device(saved, top_grad, down_weight, up_weight):
    grads, gathered, poly, norms = backward(
        *[pltpu.with_memory_space_constraint(a, pltpu.HBM) for a in (saved[0], top_grad, down_weight[0], up_weight[0])]
    )
    updates, norm_values, grads = update(poly, gathered, norms, grads)
    return grads[None], updates, norm_values


def solution(mesh):
    return jax.shard_map(
        per_device,
        mesh=mesh,
        in_specs=(
            P("section", "dp", None),
            P("dp", None),
            P("section", None, None),
            P("section", None, None),
        ),
        out_specs=(P("section", "dp", None), P("section", None, None, None), P("section", None)),
        check_vma=False,
    )
```

```python
import math

import jax
import jax.numpy as jnp
from jax import lax
from jax.experimental import pallas as pl
from jax.experimental.pallas import tpu as pltpu
from jax.sharding import PartitionSpec as P

D = 7168
LAT = 256
ITERS = 5
TOK = 128
ROWS = 16
PAIRS = TOK // ROWS
CHUNKS = 4
WIDE = D // CHUNKS
SMALL = 8
SMALLS = TOK // SMALL
PACK = D // 2
PARTS = ((0, 1024), (1024, 1024), (2048, 1024), (3072, 512))
QUARTERS = 4
READY = 3
QUARTER = LAT // QUARTERS
BLOCKS = 8
BLOCK = D // BLOCKS
PLACES = 8
PEERS = 16
Z = 4
SECTIONS = 8

norm_eps = 1e-06
frob_eps = 1e-07
coef_a = 3.4445
coef_b = -4.775
coef_c = 2.0315

MESH = pl.DeviceIdType.MESH
f32 = jnp.float32
bf16 = jnp.bfloat16
HIGHEST = lax.Precision.HIGHEST


def remote(src, dst, send, recv, device):
    return pltpu.make_async_remote_copy(
        src_ref=src, dst_ref=dst, send_sem=send, recv_sem=recv, device_id=device, device_id_type=MESH
    )


def nt_dot(a, b, precision=None):
    return lax.dot_general(
        a, b, (((1,), (1,)), ((), ())), preferred_element_type=f32, precision=precision
    )


def tn_dot(a, b):
    return lax.dot_general(a, b, (((0,), (0,)), ((), ())), preferred_element_type=f32)


def split(a):
    high = a.astype(bf16)
    return high, (a - high.astype(f32)).astype(bf16)


def dot(a, b):
    return jnp.dot(a, b, preferred_element_type=f32)


def exact_dot(a, b):
    return jnp.dot(a, b, precision=HIGHEST, preferred_element_type=f32)


def three_dot(a, b):
    (a_high, a_low), (b_high, b_low) = split(a), split(b)
    return dot(a_high, b_high) + (dot(a_high, b_low) + dot(a_low, b_high))


def newton_schulz(gram):
    total = None
    eye = diagonal_mask().astype(f32)
    for step in range(ITERS):
        mul = exact_dot if step < 1 else three_dot
        poly = coef_a * eye + coef_b * gram + coef_c * mul(gram, gram)
        if step < ITERS - 1:
            gram = mul(mul(poly, gram), poly)
        total = poly if total is None else three_dot(poly, total)
    return total


def diagonal_mask():
    return lax.broadcasted_iota(jnp.int32, (LAT, LAT), 0) == lax.broadcasted_iota(
        jnp.int32, (LAT, LAT), 1
    )


def backward_kernel(
    saved, top, w_down, w_up, grads_out, blocks, poly_out, norm_out,
    x_v, x_p, wd_v, wu_v, wut_v, normed_v, og_v, og_p, ig_v, ig_p, inv_v, latent_v, slope_v, act_v, lat_v,
    big_all, small_all, give_v, take_v,
    load_sem, wd_sem, chain_send, chain_recv, big_send, big_recv, small_send, small_recv, store_sem,
    give_send, give_recv, ring_send, ring_recv, core_send, core_recv, poly_send, poly_recv,
):
    s = lax.axis_index("section")
    d = lax.axis_index("dp")
    core = lax.rem(d, 2)
    q = lax.div(d, 2)
    x = lax.rem(q, 2)
    z = lax.div(q, 2)
    up = lax.rem(z + 1, Z)
    down = lax.rem(z + 3, Z)
    far = lax.rem(z + 2, Z)
    is_top = s == SECTIONS - 1
    has_lower = s > 0

    def device(z_at, x_at, core_at):
        return (s, z_at * 4 + x_at * 2 + core_at)

    across = device(z, 1 - x, core)
    above = device(up, x, core)
    below = device(down, x, core)
    sibling = device(z, x, 1 - core)

    loads = [
        pltpu.make_async_copy(saved, x_v, load_sem.at[0]),
        pltpu.make_async_copy(w_up, wu_v, load_sem.at[1]),
    ]
    for k in range(BLOCKS):
        part = pl.ds((k % 2) * PACK + (k // 2) * BLOCK, BLOCK)
        loads.append(
            pltpu.make_async_copy(w_down.at[:, pl.ds(k * BLOCK, BLOCK)], wd_v.at[:, part], wd_sem.at[k])
        )
    for load in loads:
        load.start()
    top_load = pltpu.make_async_copy(top, og_v, load_sem.at[2])

    @pl.when(is_top)
    def _():
        top_load.start()

    barrier = pltpu.get_barrier_semaphore()
    for k in range(1, PEERS):
        pl.semaphore_signal(
            barrier, inc=1, device_id=(s, lax.rem(d + k, PEERS)), device_id_type=MESH
        )

    @pl.when(jnp.logical_not(is_top))
    def _():
        pl.semaphore_signal(barrier, inc=1, device_id=(s + 1, d), device_id_type=MESH)

    def pack(flat, packed, i):
        rows = pl.ds(pl.multiple_of(i * ROWS, ROWS), ROWS)
        for k in range(Z):
            even = flat[rows, 2 * k * BLOCK:(2 * k + 1) * BLOCK].astype(f32)
            odd = flat[rows, (2 * k + 1) * BLOCK:(2 * k + 2) * BLOCK].astype(f32)
            cols = slice(k * BLOCK, (k + 1) * BLOCK)
            packed[2 * i, :, cols] = jnp.concatenate([even[:SMALL], odd[:SMALL]], axis=0).astype(bf16)
            packed[2 * i + 1, :, cols] = jnp.concatenate([even[SMALL:], odd[SMALL:]], axis=0).astype(bf16)

    def unpack(packed, flat, i):
        rows = pl.ds(pl.multiple_of(i * ROWS, ROWS), ROWS)
        for k in range(Z):
            cols = slice(k * BLOCK, (k + 1) * BLOCK)
            first = packed[2 * i, :, cols].astype(f32)
            second = packed[2 * i + 1, :, cols].astype(f32)
            even = jnp.concatenate([first[:SMALL], second[:SMALL]], axis=0)
            odd = jnp.concatenate([first[SMALL:], second[SMALL:]], axis=0)
            flat[rows, 2 * k * BLOCK:(2 * k + 1) * BLOCK] = even.astype(bf16)
            flat[rows, (2 * k + 1) * BLOCK:(2 * k + 2) * BLOCK] = odd.astype(bf16)

    loads[0].wait()

    def norm_rows(m, _):
        rows = pl.ds(pl.multiple_of(m * ROWS, ROWS), ROWS)
        total = jnp.zeros((ROWS, 1), f32)
        for j in range(CHUNKS):
            part = x_v[rows, j * WIDE:(j + 1) * WIDE].astype(f32)
            total += jnp.sum(part * part, axis=1, keepdims=True)
        inv = 1.0 / jnp.sqrt(total * (1.0 / D) + norm_eps)
        inv_v[rows, :] = jnp.broadcast_to(inv, (ROWS, 128))
        for j in range(CHUNKS):
            part = x_v[rows, j * WIDE:(j + 1) * WIDE].astype(f32)
            normed_v[rows, j * WIDE:(j + 1) * WIDE] = (part * inv).astype(bf16)
        return 0

    lax.fori_loop(0, PAIRS, norm_rows, 0)
    loads[1].wait()

    def turn(k, _):
        for odd in range(2):
            cols = pl.ds(pl.multiple_of((2 * k + odd) * BLOCK, BLOCK), BLOCK)
            rows = pl.ds(pl.multiple_of(k * BLOCK, BLOCK), BLOCK)
            wut_v[rows, odd * LAT:(odd + 1) * LAT] = wu_v[:, cols].T
        return 0

    lax.fori_loop(0, Z, turn, 0)
    for load in loads[2:]:
        load.wait()

    def latent_part(k, acc):
        for odd in range(2):
            cols = pl.ds(pl.multiple_of((2 * k + odd) * BLOCK, BLOCK), BLOCK)
            part = pl.ds(pl.multiple_of(odd * PACK + k * BLOCK, BLOCK), BLOCK)
            acc = acc + nt_dot(normed_v[:, cols], wd_v[:, part])
        return acc

    latent = lax.fori_loop(0, Z, latent_part, jnp.zeros((TOK, LAT), f32))
    sigmoid = 1.0 / (1.0 + jnp.exp(-latent))
    latent_v[...] = latent
    act_v[...] = (latent * sigmoid).astype(bf16)
    slope_v[...] = sigmoid * (1.0 + latent * (1.0 - sigmoid))

    @pl.when(has_lower)
    def _():
        pl.semaphore_wait(barrier, PEERS)

    @pl.when(jnp.logical_not(has_lower))
    def _():
        pl.semaphore_wait(barrier, PEERS - 1)

    place = z * 2 + core
    direct = s == 0

    def share_block(src_of, rows, target_core, act, act_own):
        for k in range(Z):
            z_at = lax.rem(z + k, Z)
            for e in range(2):
                half = lax.rem(x + e, 2)
                to_x = jnp.where(direct, half, x)
                slot = jnp.where(direct, x, half)
                src = src_of(pl.ds(pl.multiple_of((z_at * 2 + half) * BLOCK, BLOCK), BLOCK))
                dst = big_all.at[place, slot, rows]
                recv = big_recv.at[place, slot]
                copy = remote(src, dst, big_send, recv, device(z_at, to_x, target_core))
                if k:
                    act(copy)
                else:
                    away = core != target_core
                    if e:
                        away = jnp.logical_or(away, direct)

                    @pl.when(away)
                    def _():
                        act(copy)

                    if act_own is not None:

                        @pl.when(jnp.logical_not(away))
                        def _():
                            act_own(pltpu.make_async_copy(src, dst, recv))

    def share_small(src, rows, target_core, act, act_own):
        slot = jnp.where(direct, x, 0)
        dst = small_all.at[place, slot, rows]
        recv = small_recv.at[place, slot]
        for k in range(Z):
            z_at = lax.rem(z + k, Z)
            copy = remote(src, dst, small_send, recv, device(z_at, x, target_core))
            if k:
                act(copy)
            else:

                @pl.when(core != target_core)
                def _():
                    act(copy)

                if act_own is not None:

                    @pl.when(core == target_core)
                    def _():
                        act_own(pltpu.make_async_copy(src, dst, recv))

        @pl.when(direct)
        def _():
            for k in range(Z):
                z_at = lax.rem(z + k, Z)
                act(remote(src, dst, small_send, recv, device(z_at, 1 - x, target_core)))

    def begin(copy):
        copy.start()

    def left(copy):
        copy.wait_send()

    every = pl.ds(0, TOK)

    def share_normed(act, act_own):
        share_block(lambda cols: normed_v.at[:, cols], every, 0, act, act_own)
        share_small(act_v, every, 1, act, act_own)

    def share_grads(i, act, act_own):
        rows = pl.ds(pl.multiple_of(i * ROWS, ROWS), ROWS)
        share_block(lambda cols: og_v.at[rows, cols], rows, 1, act, act_own)
        share_small(lat_v.at[rows], rows, 0, act, act_own)

    @pl.when(jnp.logical_not(is_top))
    def _():
        share_normed(begin, begin)

    @pl.when(is_top)
    def _():
        top_load.wait()

    def chain_copy(m, j):
        cols = pl.ds(*PARTS[j])
        return remote(
            ig_p.at[m, :, cols], og_p.at[m, :, cols], chain_send.at[m, j], chain_recv.at[m, j],
            (jnp.maximum(s - 1, 0), d),
        )

    def receive(m):
        rows = pl.ds(pl.multiple_of(m * SMALL, SMALL), SMALL)
        acc = jnp.zeros((ROWS, 2 * LAT), f32)
        for j, (at, width) in enumerate(PARTS):

            @pl.when(jnp.logical_not(is_top))
            def _():
                chain_copy(m, j).wait_recv()

            acc += dot(og_p[m, :, at:at + width], wut_v[at:at + width, :])
        act_grad = acc[:SMALL, :LAT] + acc[SMALL:, LAT:]
        lat = (act_grad * slope_v[rows, :]).astype(bf16).astype(f32)
        inv = inv_v[rows, 0:1]
        mean = jnp.sum(lat * latent_v[rows, :], axis=1, keepdims=True) * (1.0 / D)
        pull = inv * inv * mean
        return lat, inv, pull

    def answer(m, lat, inv, pull):
        lat_twice = jnp.concatenate([lat, lat], axis=0).astype(bf16)
        inv_twice = jnp.concatenate([inv, inv], axis=0)
        pull_twice = jnp.concatenate([pull, pull], axis=0)
        for j, (at, width) in enumerate(PARTS):
            cols = slice(at, at + width)
            even = dot(lat_twice, wd_v[:, at:at + width])
            odd = dot(lat_twice, wd_v[:, PACK + at:PACK + at + width])
            ng = jnp.concatenate([even[:SMALL], odd[SMALL:]], axis=0)
            out = og_p[m, :, cols].astype(f32) + inv_twice * ng - pull_twice * x_p[m, :, cols].astype(f32)
            ig_p[m, :, cols] = out.astype(bf16)

            @pl.when(has_lower)
            def _():
                chain_copy(m, j).start()

    def micro(i, _):
        rows = pl.ds(pl.multiple_of(i * ROWS, ROWS), ROWS)
        pack(x_v, x_p, i)

        @pl.when(is_top)
        def _():
            pack(og_v, og_p, i)

        first = receive(2 * i)
        answer(2 * i, *first)
        second = receive(2 * i + 1)

        def share_pair():
            lat_v[rows, :] = jnp.concatenate([first[0], second[0]], axis=0).astype(bf16)

            @pl.when(jnp.logical_not(is_top))
            def _():
                unpack(og_p, og_v, i)

            share_grads(i, begin, begin)

        @pl.when(direct)
        def _():
            share_pair()

        answer(2 * i + 1, *second)

        @pl.when(jnp.logical_not(direct))
        def _():
            share_pair()

        unpack(ig_p, ig_v, i)
        return 0

    lax.fori_loop(0, PAIRS, micro, 0)

    @pl.when(is_top)
    def _():
        share_normed(begin, begin)

    store = pltpu.make_async_copy(ig_v, grads_out, store_sem)
    store.start()

    def arrived(p, _):
        for slot in range(2):
            part = big_all.at[p, slot]
            pltpu.make_async_copy(part, part, big_recv.at[p, slot]).wait()
        part = small_all.at[p, 0]
        pltpu.make_async_copy(part, part, small_recv.at[p, 0]).wait()
        return 0

    lax.fori_loop(0, PLACES, arrived, 0)

    @pl.when(direct)
    def _():
        def more(p, _):
            part = small_all.at[p, 1]
            pltpu.make_async_copy(part, part, small_recv.at[p, 1]).wait()
            return 0

        lax.fori_loop(0, PLACES, more, 0)

    ring_copies = []
    core_copies = []

    def quarter_rows(n):
        return pl.ds(n * QUARTER, QUARTER)

    def at(z_at, x_at, n):
        return blocks.at[core, z_at * 2 + x_at, quarter_rows(n)]

    def ring_copy(z_at, x_at, n, to, sem):
        return remote(
            at(z_at, x_at, n), at(z_at, x_at, n), ring_send.at[sem], ring_recv.at[z_at * 2 + x_at, n], to
        )

    def forward(z_at, x_at, n, to):
        copy = ring_copy(z_at, x_at, n, to, 3 * QUARTERS + len(ring_copies))
        copy.start()
        ring_copies.append(copy)

    def core_copy(z_at, x_at, n):
        return remote(
            at(z_at, x_at, n), at(z_at, x_at, n), core_send, core_recv, sibling
        )

    def to_sibling(z_at, x_at, n):
        copy = core_copy(z_at, x_at, n)
        copy.start()
        core_copies.append(copy)

    def wait(z_at, x_at, n):
        part = at(z_at, x_at, n)
        pltpu.make_async_copy(part, part, ring_recv.at[z_at * 2 + x_at, n]).wait()

    def used(z_at, x_at):
        part = blocks[core, z_at * 2 + x_at]
        return nt_dot(part, part)

    def own_copies(n):
        return [ring_copy(z, x, n, to, 3 * n + k) for k, to in enumerate((above, below, across))] + [
            core_copy(z, x, n)
        ]

    def send_own(n):
        for copy in own_copies(n):
            copy.start()

    @pl.when(direct)
    def _():
        turned = small_all[...].reshape(2 * PLACES * TOK, LAT).T
        right = big_all[...].reshape(2 * PLACES * TOK, BLOCK)
        for n in range(QUARTERS):
            blocks[core, q, quarter_rows(n)] = dot(turned[n * QUARTER:(n + 1) * QUARTER], right).astype(bf16)
            send_own(n)

    def give_copy(n):
        return remote(
            give_v.at[quarter_rows(n)], take_v.at[quarter_rows(n)], give_send.at[n], give_recv.at[n], across
        )

    @pl.when(jnp.logical_not(direct))
    def _():
        turned = small_all[:, 0].reshape(PLACES * TOK, LAT).T
        right = big_all[:, 1 - x].reshape(PLACES * TOK, BLOCK)
        for n in range(QUARTERS):
            give_v[quarter_rows(n)] = dot(turned[n * QUARTER:(n + 1) * QUARTER], right).astype(bf16)
            give_copy(n).start()
        mine = dot(turned, big_all[:, x].reshape(PLACES * TOK, BLOCK))
        for n in range(QUARTERS):
            give_copy(n).wait_recv()
            total = mine[n * QUARTER:(n + 1) * QUARTER] + take_v[quarter_rows(n)].astype(f32)
            blocks[core, q, quarter_rows(n)] = total.astype(bf16)
            send_own(n)
        for n in range(QUARTERS):
            give_copy(n).wait_send()

    gram = used(z, x)
    for n in range(QUARTERS):
        wait(down, x, n)
        if n < QUARTERS // 2:
            forward(down, x, n, above)
        to_sibling(down, x, n)
        wait(up, x, n)
        if n >= QUARTERS // 2:
            forward(up, x, n, below)
        to_sibling(up, x, n)
        wait(z, 1 - x, n)
        forward(z, 1 - x, n, above)
        forward(z, 1 - x, n, below)
        to_sibling(z, 1 - x, n)
    gram += used(down, x)
    gram += used(up, x)
    gram += used(z, 1 - x)
    for n in (0, 2, 1, 3):
        wait(far, x, n)
        forward(far, x, n, across)
        to_sibling(far, x, n)
    gram += used(far, x)
    for n in range(QUARTERS):
        for z_at in (up, down):
            wait(z_at, 1 - x, n)
            to_sibling(z_at, 1 - x, n)
    gram += used(up, 1 - x)
    gram += used(down, 1 - x)
    for n in (0, 2, 1, 3):
        wait(far, 1 - x, n)
        to_sibling(far, 1 - x, n)
    gram += used(far, 1 - x)

    squares = jnp.where(diagonal_mask(), gram, 0.0)
    norm = jnp.sqrt(jnp.sum(jnp.sum(squares, axis=1, keepdims=True), axis=0, keepdims=True))
    scale = 1.0 / (norm + frob_eps)
    poly = newton_schulz(gram * scale * scale) * (scale * (0.2 * math.sqrt(D)))
    high, low = split(poly)
    poly_out[core, 0] = high
    poly_out[core, 1] = low
    norm_out[core] = jnp.broadcast_to(norm, (8, 128))
    polys = [
        remote(poly_out.at[core], poly_out.at[core], poly_send.at[0], poly_recv.at[0], sibling),
        remote(norm_out.at[core], norm_out.at[core], poly_send.at[1], poly_recv.at[1], sibling),
    ]
    for copy in polys:
        copy.start()

    for n in range(QUARTERS):
        for copy in own_copies(n):
            copy.wait_send()
    for copy in ring_copies + core_copies:
        copy.wait_send()

    def finish(j, _):
        right = blocks[core, j]
        blocks[core, j] = (dot(high, right) + dot(low, right)).astype(bf16)
        return 0

    lax.fori_loop(0, READY, finish, 0)
    theirs = 1 - core
    pltpu.make_async_copy(blocks.at[theirs], blocks.at[theirs], core_recv).wait()
    pltpu.make_async_copy(poly_out.at[theirs], poly_out.at[theirs], poly_recv.at[0]).wait()
    pltpu.make_async_copy(norm_out.at[theirs], norm_out.at[theirs], poly_recv.at[1]).wait()

    share_normed(left, None)

    def sent(m, _):
        share_grads(m, left, None)

        @pl.when(has_lower)
        def _():
            for j in range(len(PARTS)):
                chain_copy(2 * m, j).wait_send()
                chain_copy(2 * m + 1, j).wait_send()

        return 0

    lax.fori_loop(0, PAIRS, sent, 0)
    for copy in polys:
        copy.wait_send()
    store.wait()


def backward(saved, top, w_down, w_up):
    hbm = pl.BlockSpec(memory_space=pl.ANY)
    vmem = pl.BlockSpec(memory_space=pltpu.VMEM)
    dma = pltpu.SemaphoreType.DMA
    return pl.pallas_call(
        backward_kernel,
        out_shape=(
            pltpu.VMEM((TOK, D), bf16),
            pltpu.VMEM((2, BLOCKS, LAT, BLOCK), bf16),
            pltpu.VMEM((2, 2, LAT, LAT), bf16),
            pltpu.VMEM((2, 8, 128), f32),
        ),
        in_specs=[hbm] * 4,
        out_specs=(hbm, vmem, vmem, vmem),
        scratch_shapes=[
            pltpu.VMEM((TOK, D), bf16),
            pltpu.VMEM((SMALLS, ROWS, PACK), bf16),
            pltpu.VMEM((LAT, D), bf16),
            pltpu.VMEM((LAT, D), bf16),
            pltpu.VMEM((PACK, 2 * LAT), bf16),
            pltpu.VMEM((TOK, D), bf16),
            pltpu.VMEM((TOK, D), bf16),
            pltpu.VMEM((SMALLS, ROWS, PACK), bf16),
            pltpu.VMEM((TOK, D), bf16),
            pltpu.VMEM((SMALLS, ROWS, PACK), bf16),
            pltpu.VMEM((TOK, 128), f32),
            pltpu.VMEM((TOK, LAT), f32),
            pltpu.VMEM((TOK, LAT), f32),
            pltpu.VMEM((TOK, LAT), bf16),
            pltpu.VMEM((TOK, LAT), bf16),
            pltpu.VMEM((PLACES, 2, TOK, BLOCK), bf16),
            pltpu.VMEM((PLACES, 2, TOK, LAT), bf16),
            pltpu.VMEM((LAT, BLOCK), bf16),
            pltpu.VMEM((LAT, BLOCK), bf16),
            dma((3,)),
            dma((BLOCKS,)),
            dma((SMALLS, len(PARTS))),
            dma((SMALLS, len(PARTS))),
            dma(()),
            dma((PLACES, 2)),
            dma(()),
            dma((PLACES, 2)),
            dma(()),
            dma((QUARTERS,)),
            dma((QUARTERS,)),
            dma((7 * QUARTERS,)),
            dma((BLOCKS, QUARTERS)),
            dma(()),
            dma(()),
            dma((2,)),
            dma((2,)),
        ],
        name="backward",
        compiler_params=pltpu.CompilerParams(
            collective_id=0, has_side_effects=True, vmem_limit_bytes=40 * 2**20
        ),
    )(saved, top, w_down, w_up)


def update_kernel(poly, blocks, norms, grads, out, norm_out, grads_out, stage, store_sem):
    mine = lax.rem(lax.axis_index("dp"), 2)
    theirs = 1 - mine
    stores = []

    def store(src, dst):
        copy = pltpu.make_async_copy(src, dst, store_sem.at[len(stores)])
        copy.start()
        stores.append(copy)

    for j in range(READY):
        store(blocks.at[mine, j], out.at[0, mine, :, pl.ds(j * BLOCK, BLOCK)])
    store(grads, grads_out)
    column = lax.broadcasted_iota(jnp.int32, (1, 2), 1)
    norm_out[...] = jnp.where(column == 0, norms[0, 0:1, 0:1], norms[1, 0:1, 0:1])
    todo = [(mine, j) for j in range(READY, BLOCKS)] + [(theirs, j) for j in range(BLOCKS)]
    for n, (i, j) in enumerate(todo):
        right = blocks[i, j]
        stage[n] = (dot(poly[i, 0], right) + dot(poly[i, 1], right)).astype(bf16)
        store(stage.at[n], out.at[0, i, :, pl.ds(j * BLOCK, BLOCK)])
    for copy in stores:
        copy.wait()


def update(poly, blocks, norms, grads):
    hbm = pl.BlockSpec(memory_space=pl.ANY)
    vmem = pl.BlockSpec(memory_space=pltpu.VMEM)
    return pl.pallas_call(
        update_kernel,
        out_shape=(
            jax.ShapeDtypeStruct((1, 2, LAT, D), bf16),
            jax.ShapeDtypeStruct((1, 2), f32),
            jax.ShapeDtypeStruct((TOK, D), bf16),
        ),
        in_specs=[vmem] * 4,
        out_specs=(hbm, vmem, hbm),
        scratch_shapes=[
            pltpu.VMEM((2 * BLOCKS - READY, LAT, BLOCK), bf16),
            pltpu.SemaphoreType.DMA((2 * BLOCKS + 1,)),
        ],
        name="update",
        compiler_params=pltpu.CompilerParams(vmem_limit_bytes=30 * 2**20),
    )(*[pltpu.with_memory_space_constraint(a, pltpu.VMEM) for a in (poly, blocks, norms, grads)])


def per_device(saved, top_grad, down_weight, up_weight):
    grads, blocks, poly, norms = backward(
        *[pltpu.with_memory_space_constraint(a, pltpu.HBM) for a in (saved[0], top_grad, down_weight[0], up_weight[0])]
    )
    updates, norm_values, grads = update(poly, blocks, norms, grads)
    return grads[None], updates, norm_values


def solution(mesh):
    return jax.shard_map(
        per_device,
        mesh=mesh,
        in_specs=(
            P("section", "dp", None),
            P("dp", None),
            P("section", None, None),
            P("section", None, None),
        ),
        out_specs=(P("section", "dp", None), P("section", None, None, None), P("section", None)),
        check_vma=False,
    )
```

```python
import math

import jax
import jax.numpy as jnp
from jax import lax
from jax.experimental import pallas as pl
from jax.experimental.pallas import tpu as pltpu
from jax.sharding import PartitionSpec as P

D = 7168
LAT = 256
SECTIONS = 8
ITERS = 5
TOK = 128
ROWS = 16
PAIRS = TOK // ROWS
CHUNKS = 4
WIDE = D // CHUNKS
SMALL = 8
SMALLS = TOK // SMALL
PACK = D // 2
PARTS = ((0, 1024), (1024, 1024), (2048, 1024), (3072, 512))
READY = 3
PIECES = ((0, 64), (64, 64), (128, 80), (208, 48))
QUARTERS = len(PIECES)
LAST = QUARTERS - 1
ORDER = (LAST, 0, 1, 2)
HELPED = 2
APART = SECTIONS - HELPED
BLOCKS = 8
BLOCK = D // BLOCKS
PLACES = 8
PEERS = 16
Z = 4

norm_eps = 1e-06
frob_eps = 1e-07
coef_a = 3.4445
coef_b = -4.775
coef_c = 2.0315

MESH = pl.DeviceIdType.MESH
f32 = jnp.float32
bf16 = jnp.bfloat16


def remote(src, dst, send, recv, device):
    return pltpu.make_async_remote_copy(
        src_ref=src, dst_ref=dst, send_sem=send, recv_sem=recv, device_id=device, device_id_type=MESH
    )


def nt_dot(a, b):
    return lax.dot_general(
        a, b, (((1,), (1,)), ((), ())), preferred_element_type=f32
    )


def tn_dot(a, b):
    return lax.dot_general(a, b, (((0,), (0,)), ((), ())), preferred_element_type=f32)


def split(a):
    high = a.astype(bf16)
    return high, (a - high.astype(f32)).astype(bf16)


def dot(a, b):
    return jnp.dot(a, b, preferred_element_type=f32)


def three_dot(a, b):
    (a_high, a_low), (b_high, b_low) = split(a), split(b)
    return dot(a_high, b_high) + (dot(a_high, b_low) + dot(a_low, b_high))


def newton_schulz(gram):
    total = None
    eye = diagonal_mask().astype(f32)
    for step in range(ITERS):
        poly = coef_a * eye + coef_b * gram + coef_c * three_dot(gram, gram)
        if step < ITERS - 1:
            gram = three_dot(three_dot(poly, gram), poly)
        total = poly if total is None else three_dot(poly, total)
    return total


def diagonal_mask():
    return lax.broadcasted_iota(jnp.int32, (LAT, LAT), 0) == lax.broadcasted_iota(
        jnp.int32, (LAT, LAT), 1
    )


def backward_kernel(
    saved, top, w_down, w_up, grads_out, blocks, poly_out, norm_out,
    x_v, x_p, wd_v, wu_v, wut_v, normed_v, og_v, og_p, ig_v, ig_p, inv_v, latent_v, slope_v, act_v, lat_v,
    big_all, small_all, give_v, take_v, relay,
    load_sem, wd_sem, chain_send, chain_recv, big_send, big_recv, small_send, small_recv, store_sem,
    give_send, give_recv, ring_send, ring_recv, core_send, core_recv, poly_send, poly_recv, relay_send, relay_recv,
):
    s = lax.axis_index("section")
    d = lax.axis_index("dp")
    core = lax.rem(d, 2)
    q = lax.div(d, 2)
    x = lax.rem(q, 2)
    z = lax.div(q, 2)
    up = lax.rem(z + 1, Z)
    down = lax.rem(z + 3, Z)
    far = lax.rem(z + 2, Z)
    is_top = s == SECTIONS - 1
    has_lower = s > 0

    def device(z_at, x_at, core_at):
        return (s, z_at * 4 + x_at * 2 + core_at)

    across = device(z, 1 - x, core)
    above = device(up, x, core)
    below = device(down, x, core)
    sibling = device(z, x, 1 - core)

    loads = [
        pltpu.make_async_copy(saved, x_v, load_sem.at[0]),
        pltpu.make_async_copy(w_up, wu_v, load_sem.at[1]),
    ]
    for k in range(BLOCKS):
        part = pl.ds((k % 2) * PACK + (k // 2) * BLOCK, BLOCK)
        loads.append(
            pltpu.make_async_copy(w_down.at[:, pl.ds(k * BLOCK, BLOCK)], wd_v.at[:, part], wd_sem.at[k])
        )
    for load in loads:
        load.start()
    top_load = pltpu.make_async_copy(top, og_v, load_sem.at[2])

    @pl.when(is_top)
    def _():
        top_load.start()

    barrier = pltpu.get_barrier_semaphore()
    for k in range(1, PEERS):
        pl.semaphore_signal(
            barrier, inc=1, device_id=(s, lax.rem(d + k, PEERS)), device_id_type=MESH
        )

    @pl.when(jnp.logical_not(is_top))
    def _():
        pl.semaphore_signal(barrier, inc=1, device_id=(s + 1, d), device_id_type=MESH)

    def pack(flat, packed, i):
        rows = pl.ds(pl.multiple_of(i * ROWS, ROWS), ROWS)
        for k in range(Z):
            even = flat[rows, 2 * k * BLOCK:(2 * k + 1) * BLOCK].astype(f32)
            odd = flat[rows, (2 * k + 1) * BLOCK:(2 * k + 2) * BLOCK].astype(f32)
            cols = slice(k * BLOCK, (k + 1) * BLOCK)
            packed[2 * i, :, cols] = jnp.concatenate([even[:SMALL], odd[:SMALL]], axis=0).astype(bf16)
            packed[2 * i + 1, :, cols] = jnp.concatenate([even[SMALL:], odd[SMALL:]], axis=0).astype(bf16)

    def unpack(packed, flat, i):
        rows = pl.ds(pl.multiple_of(i * ROWS, ROWS), ROWS)
        for k in range(Z):
            cols = slice(k * BLOCK, (k + 1) * BLOCK)
            first = packed[2 * i, :, cols].astype(f32)
            second = packed[2 * i + 1, :, cols].astype(f32)
            even = jnp.concatenate([first[:SMALL], second[:SMALL]], axis=0)
            odd = jnp.concatenate([first[SMALL:], second[SMALL:]], axis=0)
            flat[rows, 2 * k * BLOCK:(2 * k + 1) * BLOCK] = even.astype(bf16)
            flat[rows, (2 * k + 1) * BLOCK:(2 * k + 2) * BLOCK] = odd.astype(bf16)

    helped = s < HELPED
    helper = s >= APART
    partner = (jnp.where(helped, s + APART, jnp.where(helper, s - APART, s)), d)

    @pl.when(jnp.logical_or(helped, helper))
    def _():
        pl.semaphore_signal(barrier, inc=1, device_id=partner, device_id_type=MESH)

    loads[0].wait()

    def norm_rows(m, _):
        rows = pl.ds(pl.multiple_of(m * ROWS, ROWS), ROWS)
        total = jnp.zeros((ROWS, 1), f32)
        for j in range(CHUNKS):
            part = x_v[rows, j * WIDE:(j + 1) * WIDE].astype(f32)
            total += jnp.sum(part * part, axis=1, keepdims=True)
        inv = 1.0 / jnp.sqrt(total * (1.0 / D) + norm_eps)
        inv_v[rows, :] = jnp.broadcast_to(inv, (ROWS, 128))
        for j in range(CHUNKS):
            part = x_v[rows, j * WIDE:(j + 1) * WIDE].astype(f32)
            normed_v[rows, j * WIDE:(j + 1) * WIDE] = (part * inv).astype(bf16)
        return 0

    lax.fori_loop(0, PAIRS, norm_rows, 0)
    loads[1].wait()

    def turn(k, _):
        for odd in range(2):
            cols = pl.ds(pl.multiple_of((2 * k + odd) * BLOCK, BLOCK), BLOCK)
            rows = pl.ds(pl.multiple_of(k * BLOCK, BLOCK), BLOCK)
            wut_v[rows, odd * LAT:(odd + 1) * LAT] = wu_v[:, cols].T
        return 0

    lax.fori_loop(0, Z, turn, 0)
    for load in loads[2:]:
        load.wait()

    def latent_part(k, acc):
        for odd in range(2):
            cols = pl.ds(pl.multiple_of((2 * k + odd) * BLOCK, BLOCK), BLOCK)
            part = pl.ds(pl.multiple_of(odd * PACK + k * BLOCK, BLOCK), BLOCK)
            acc = acc + nt_dot(normed_v[:, cols], wd_v[:, part])
        return acc

    latent = lax.fori_loop(0, Z, latent_part, jnp.zeros((TOK, LAT), f32))
    sigmoid = 1.0 / (1.0 + jnp.exp(-latent))
    latent_v[...] = latent
    act_v[...] = (latent * sigmoid).astype(bf16)
    slope_v[...] = sigmoid * (1.0 + latent * (1.0 - sigmoid))

    both = jnp.logical_and(has_lower, jnp.logical_or(helped, helper))

    @pl.when(both)
    def _():
        pl.semaphore_wait(barrier, PEERS + 1)

    @pl.when(jnp.logical_not(both))
    def _():
        pl.semaphore_wait(barrier, PEERS)

    place = z * 2 + core
    direct = s == 0

    def share_block(src_of, rows, target_core, act, act_own):
        for k in range(Z):
            z_at = lax.rem(z + k, Z)
            for e in range(2):
                half = lax.rem(x + e, 2)
                to_x = jnp.where(direct, half, x)
                slot = jnp.where(direct, x, half)
                src = src_of(pl.ds(pl.multiple_of((z_at * 2 + half) * BLOCK, BLOCK), BLOCK))
                dst = big_all.at[place, slot, rows]
                recv = big_recv.at[place, slot]
                copy = remote(src, dst, big_send, recv, device(z_at, to_x, target_core))
                if k:
                    act(copy)
                else:
                    away = core != target_core
                    if e:
                        away = jnp.logical_or(away, direct)

                    @pl.when(away)
                    def _():
                        act(copy)

                    if act_own is not None:

                        @pl.when(jnp.logical_not(away))
                        def _():
                            act_own(pltpu.make_async_copy(src, dst, recv))

    def share_small(src, rows, target_core, act, act_own):
        slot = jnp.where(direct, x, 0)
        dst = small_all.at[place, slot, rows]
        recv = small_recv.at[place, slot]
        for k in range(Z):
            z_at = lax.rem(z + k, Z)
            copy = remote(src, dst, small_send, recv, device(z_at, x, target_core))
            if k:
                act(copy)
            else:

                @pl.when(core != target_core)
                def _():
                    act(copy)

                if act_own is not None:

                    @pl.when(core == target_core)
                    def _():
                        act_own(pltpu.make_async_copy(src, dst, recv))

        @pl.when(direct)
        def _():
            for k in range(Z):
                z_at = lax.rem(z + k, Z)
                act(remote(src, dst, small_send, recv, device(z_at, 1 - x, target_core)))

    def begin(copy):
        copy.start()

    def left(copy):
        copy.wait_send()

    every = pl.ds(0, TOK)

    def share_normed(act, act_own):
        share_block(lambda cols: normed_v.at[:, cols], every, 0, act, act_own)
        share_small(act_v, every, 1, act, act_own)

    def share_grads(i, act, act_own):
        rows = pl.ds(pl.multiple_of(i * ROWS, ROWS), ROWS)
        share_block(lambda cols: og_v.at[rows, cols], rows, 1, act, act_own)
        share_small(lat_v.at[rows], rows, 0, act, act_own)

    @pl.when(jnp.logical_not(is_top))
    def _():
        share_normed(begin, begin)

    @pl.when(is_top)
    def _():
        top_load.wait()

    def chain_copy(m, j):
        cols = pl.ds(*PARTS[j])
        return remote(
            ig_p.at[m, :, cols], og_p.at[m, :, cols], chain_send.at[m, j], chain_recv.at[m, j],
            (jnp.maximum(s - 1, 0), d),
        )

    def receive(m):
        rows = pl.ds(pl.multiple_of(m * SMALL, SMALL), SMALL)
        acc = jnp.zeros((ROWS, 2 * LAT), f32)
        for j, (at, width) in enumerate(PARTS):

            @pl.when(jnp.logical_not(is_top))
            def _():
                chain_copy(m, j).wait_recv()

            acc += dot(og_p[m, :, at:at + width], wut_v[at:at + width, :])
        act_grad = acc[:SMALL, :LAT] + acc[SMALL:, LAT:]
        lat = (act_grad * slope_v[rows, :]).astype(bf16).astype(f32)
        inv = inv_v[rows, 0:1]
        mean = jnp.sum(lat * latent_v[rows, :], axis=1, keepdims=True) * (1.0 / D)
        pull = inv * inv * mean
        return lat, inv, pull

    def answer(m, lat, inv, pull):
        lat_twice = jnp.concatenate([lat, lat], axis=0).astype(bf16)
        inv_twice = jnp.concatenate([inv, inv], axis=0)
        pull_twice = jnp.concatenate([pull, pull], axis=0)
        for j, (at, width) in enumerate(PARTS):
            cols = slice(at, at + width)
            even = dot(lat_twice, wd_v[:, at:at + width])
            odd = dot(lat_twice, wd_v[:, PACK + at:PACK + at + width])
            ng = jnp.concatenate([even[:SMALL], odd[SMALL:]], axis=0)
            out = og_p[m, :, cols].astype(f32) + inv_twice * ng - pull_twice * x_p[m, :, cols].astype(f32)
            ig_p[m, :, cols] = out.astype(bf16)

            @pl.when(has_lower)
            def _():
                chain_copy(m, j).start()

    def micro(i, _):
        rows = pl.ds(pl.multiple_of(i * ROWS, ROWS), ROWS)
        pack(x_v, x_p, i)

        @pl.when(is_top)
        def _():
            pack(og_v, og_p, i)

        @pl.when(jnp.logical_and(is_top, i == 1))
        def _():
            share_normed(begin, begin)

        first = receive(2 * i)
        answer(2 * i, *first)
        second = receive(2 * i + 1)

        def share_pair():
            lat_v[rows, :] = jnp.concatenate([first[0], second[0]], axis=0).astype(bf16)

            @pl.when(jnp.logical_not(is_top))
            def _():
                unpack(og_p, og_v, i)

            share_grads(i, begin, begin)

        @pl.when(direct)
        def _():
            share_pair()

        answer(2 * i + 1, *second)

        @pl.when(jnp.logical_not(direct))
        def _():
            share_pair()

        unpack(ig_p, ig_v, i)
        return 0

    lax.fori_loop(0, PAIRS, micro, 0)

    store = pltpu.make_async_copy(ig_v, grads_out, store_sem)
    store.start()

    def arrived(p, _):
        for slot in range(2):
            part = big_all.at[p, slot]
            pltpu.make_async_copy(part, part, big_recv.at[p, slot]).wait()
        part = small_all.at[p, 0]
        pltpu.make_async_copy(part, part, small_recv.at[p, 0]).wait()
        return 0

    lax.fori_loop(0, PLACES, arrived, 0)

    @pl.when(direct)
    def _():
        def more(p, _):
            part = small_all.at[p, 1]
            pltpu.make_async_copy(part, part, small_recv.at[p, 1]).wait()
            return 0

        lax.fori_loop(0, PLACES, more, 0)

    ring_copies = []
    alone_copies = []
    core_copies = []

    def quarter_rows(n):
        return pl.ds(*PIECES[n])

    def piece(n):
        return slice(PIECES[n][0], PIECES[n][0] + PIECES[n][1])

    def at(z_at, x_at, n):
        return blocks.at[core, z_at * 2 + x_at, quarter_rows(n)]

    def ring_copy(z_at, x_at, n, to, sem):
        return remote(
            at(z_at, x_at, n), at(z_at, x_at, n), ring_send.at[sem], ring_recv.at[z_at * 2 + x_at, n], to
        )

    def forward(z_at, x_at, n, to):
        copy = ring_copy(z_at, x_at, n, to, 3 * QUARTERS + len(ring_copies) + len(alone_copies))
        if n == LAST:
            alone_copies.append(copy)

            @pl.when(jnp.logical_not(helped))
            def _():
                copy.start()
        else:
            copy.start()
            ring_copies.append(copy)

    def core_copy(z_at, x_at, n):
        return remote(
            at(z_at, x_at, n), at(z_at, x_at, n), core_send, core_recv, sibling
        )

    def to_sibling(z_at, x_at, n):
        copy = core_copy(z_at, x_at, n)
        copy.start()
        core_copies.append(copy)

    def wait(z_at, x_at, n):
        part = at(z_at, x_at, n)
        pltpu.make_async_copy(part, part, ring_recv.at[z_at * 2 + x_at, n]).wait()

    def used(z_at, x_at):
        part = blocks[core, z_at * 2 + x_at]
        return nt_dot(part, part)

    def own_copies(n, act):
        copies = [ring_copy(z, x, n, to, 3 * n + k) for k, to in enumerate((above, below, across))]
        act(core_copy(z, x, n))
        if n != LAST:
            for copy in copies:
                act(copy)
        else:

            @pl.when(jnp.logical_not(helped))
            def _():
                for copy in copies:
                    act(copy)

            @pl.when(helped)
            def _():
                act(remote(at(z, x, n), relay.at[q], relay_send.at[0], relay_recv.at[q], partner))

    @pl.when(direct)
    def _():
        turned = small_all[...].reshape(2 * PLACES * TOK, LAT).T
        right = big_all[...].reshape(2 * PLACES * TOK, BLOCK)
        for n in ORDER:
            blocks[core, q, quarter_rows(n)] = dot(turned[piece(n)], right).astype(bf16)
            own_copies(n, begin)

    def give_copy(n):
        return remote(
            give_v.at[quarter_rows(n)], take_v.at[quarter_rows(n)], give_send.at[n], give_recv.at[n], across
        )

    @pl.when(jnp.logical_not(direct))
    def _():
        turned = small_all[:, 0].reshape(PLACES * TOK, LAT).T
        right = big_all[:, 1 - x].reshape(PLACES * TOK, BLOCK)
        for n in ORDER:
            give_v[quarter_rows(n)] = dot(turned[piece(n)], right).astype(bf16)
            give_copy(n).start()
        mine = dot(turned, big_all[:, x].reshape(PLACES * TOK, BLOCK))
        for n in ORDER:
            give_copy(n).wait_recv()
            total = mine[piece(n)] + take_v[quarter_rows(n)].astype(f32)
            blocks[core, q, quarter_rows(n)] = total.astype(bf16)
            own_copies(n, begin)
        for n in range(QUARTERS):
            give_copy(n).wait_send()

    def near(n):
        wait(down, x, n)
        if n < QUARTERS // 2:
            forward(down, x, n, above)
        to_sibling(down, x, n)
        wait(up, x, n)
        if n >= QUARTERS // 2:
            forward(up, x, n, below)
        to_sibling(up, x, n)
        wait(z, 1 - x, n)
        forward(z, 1 - x, n, above)
        forward(z, 1 - x, n, below)
        to_sibling(z, 1 - x, n)

    def opposite(n):
        wait(far, x, n)
        forward(far, x, n, across)
        to_sibling(far, x, n)

    gram = used(z, x)
    for n in range(LAST):
        near(n)
    for n in (0, 2, 1):
        opposite(n)
    near(LAST)
    opposite(LAST)
    gram += used(down, x)
    gram += used(up, x)
    gram += used(z, 1 - x)
    gram += used(far, x)
    for n in range(QUARTERS):
        for z_at in (up, down):
            wait(z_at, 1 - x, n)
            to_sibling(z_at, 1 - x, n)
    gram += used(up, 1 - x)
    gram += used(down, 1 - x)
    for n in (0, 2, 1, 3):
        wait(far, 1 - x, n)
        to_sibling(far, 1 - x, n)
    gram += used(far, 1 - x)

    squares = jnp.where(diagonal_mask(), gram, 0.0)
    norm = jnp.sqrt(jnp.sum(jnp.sum(squares, axis=1, keepdims=True), axis=0, keepdims=True))
    scale = 1.0 / (norm + frob_eps)
    poly = newton_schulz(gram * scale * scale) * (scale * (0.2 * math.sqrt(D)))
    high, low = split(poly)
    poly_out[core, 0] = high
    poly_out[core, 1] = low
    norm_out[core] = jnp.broadcast_to(norm, (8, 128))
    polys = [
        remote(poly_out.at[core], poly_out.at[core], poly_send.at[0], poly_recv.at[0], sibling),
        remote(norm_out.at[core], norm_out.at[core], poly_send.at[1], poly_recv.at[1], sibling),
    ]
    for copy in polys:
        copy.start()

    for n in range(QUARTERS):
        own_copies(n, left)
    for copy in ring_copies + core_copies:
        copy.wait_send()

    @pl.when(jnp.logical_not(helped))
    def _():
        for copy in alone_copies:
            copy.wait_send()

    def finish(j, _):
        right = blocks[core, j]
        blocks[core, j] = (dot(high, right) + dot(low, right)).astype(bf16)
        return 0

    lax.fori_loop(0, READY, finish, 0)
    theirs = 1 - core
    pltpu.make_async_copy(blocks.at[theirs], blocks.at[theirs], core_recv).wait()
    pltpu.make_async_copy(poly_out.at[theirs], poly_out.at[theirs], poly_recv.at[0]).wait()
    pltpu.make_async_copy(norm_out.at[theirs], norm_out.at[theirs], poly_recv.at[1]).wait()

    @pl.when(helper)
    def _():
        relays = []

        def pass_to(z_at, x_at, to):
            n = z_at * 2 + x_at
            copy = remote(relay.at[n], relay.at[n], relay_send.at[len(relays)], relay_recv.at[n], to)
            copy.start()
            relays.append(copy)

        def arrive(z_at, x_at):
            n = z_at * 2 + x_at
            pltpu.make_async_copy(relay.at[n], relay.at[n], relay_recv.at[n]).wait()

        def deliver(z_at, x_at):
            n = z_at * 2 + x_at
            copy = remote(
                relay.at[n], blocks.at[core, n, quarter_rows(LAST)],
                relay_send.at[len(relays)], ring_recv.at[n, LAST], partner,
            )
            copy.start()
            relays.append(copy)

        arrive(z, x)
        pass_to(z, x, above)
        pass_to(z, x, below)
        pass_to(z, x, across)
        arrive(down, x)
        pass_to(down, x, above)
        deliver(down, x)
        arrive(up, x)
        deliver(up, x)
        arrive(z, 1 - x)
        pass_to(z, 1 - x, above)
        pass_to(z, 1 - x, below)
        deliver(z, 1 - x)
        arrive(far, x)
        pass_to(far, x, across)
        deliver(far, x)
        for z_at in (up, down, far):
            arrive(z_at, 1 - x)
            deliver(z_at, 1 - x)
        for copy in relays:
            copy.wait_send()

    share_normed(left, None)

    def sent(m, _):
        share_grads(m, left, None)

        @pl.when(has_lower)
        def _():
            for j in range(len(PARTS)):
                chain_copy(2 * m, j).wait_send()
                chain_copy(2 * m + 1, j).wait_send()

        return 0

    lax.fori_loop(0, PAIRS, sent, 0)
    for copy in polys:
        copy.wait_send()
    store.wait()


def backward(saved, top, w_down, w_up):
    hbm = pl.BlockSpec(memory_space=pl.ANY)
    vmem = pl.BlockSpec(memory_space=pltpu.VMEM)
    dma = pltpu.SemaphoreType.DMA
    return pl.pallas_call(
        backward_kernel,
        out_shape=(
            pltpu.VMEM((TOK, D), bf16),
            pltpu.VMEM((2, BLOCKS, LAT, BLOCK), bf16),
            pltpu.VMEM((2, 2, LAT, LAT), bf16),
            pltpu.VMEM((2, 8, 128), f32),
        ),
        in_specs=[hbm] * 4,
        out_specs=(hbm, vmem, vmem, vmem),
        scratch_shapes=[
            pltpu.VMEM((TOK, D), bf16),
            pltpu.VMEM((SMALLS, ROWS, PACK), bf16),
            pltpu.VMEM((LAT, D), bf16),
            pltpu.VMEM((LAT, D), bf16),
            pltpu.VMEM((PACK, 2 * LAT), bf16),
            pltpu.VMEM((TOK, D), bf16),
            pltpu.VMEM((TOK, D), bf16),
            pltpu.VMEM((SMALLS, ROWS, PACK), bf16),
            pltpu.VMEM((TOK, D), bf16),
            pltpu.VMEM((SMALLS, ROWS, PACK), bf16),
            pltpu.VMEM((TOK, 128), f32),
            pltpu.VMEM((TOK, LAT), f32),
            pltpu.VMEM((TOK, LAT), f32),
            pltpu.VMEM((TOK, LAT), bf16),
            pltpu.VMEM((TOK, LAT), bf16),
            pltpu.VMEM((PLACES, 2, TOK, BLOCK), bf16),
            pltpu.VMEM((PLACES, 2, TOK, LAT), bf16),
            pltpu.VMEM((LAT, BLOCK), bf16),
            pltpu.VMEM((LAT, BLOCK), bf16),
            pltpu.VMEM((BLOCKS, PIECES[LAST][1], BLOCK), bf16),
            dma((3,)),
            dma((BLOCKS,)),
            dma((SMALLS, len(PARTS))),
            dma((SMALLS, len(PARTS))),
            dma(()),
            dma((PLACES, 2)),
            dma(()),
            dma((PLACES, 2)),
            dma(()),
            dma((QUARTERS,)),
            dma((QUARTERS,)),
            dma((7 * QUARTERS,)),
            dma((BLOCKS, QUARTERS)),
            dma(()),
            dma(()),
            dma((2,)),
            dma((2,)),
            dma((14,)),
            dma((BLOCKS,)),
        ],
        name="backward",
        compiler_params=pltpu.CompilerParams(
            collective_id=0, has_side_effects=True, vmem_limit_bytes=40 * 2**20
        ),
    )(saved, top, w_down, w_up)


def update_kernel(poly, blocks, norms, grads, out, norm_out, grads_out, stage, store_sem):
    mine = lax.rem(lax.axis_index("dp"), 2)
    theirs = 1 - mine
    stores = []

    def store(src, dst):
        copy = pltpu.make_async_copy(src, dst, store_sem.at[len(stores)])
        copy.start()
        stores.append(copy)

    for j in range(READY):
        store(blocks.at[mine, j], out.at[0, mine, :, pl.ds(j * BLOCK, BLOCK)])
    store(grads, grads_out)
    column = lax.broadcasted_iota(jnp.int32, (1, 2), 1)
    norm_out[...] = jnp.where(column == 0, norms[0, 0:1, 0:1], norms[1, 0:1, 0:1])
    todo = [(mine, j) for j in range(READY, BLOCKS)] + [(theirs, j) for j in range(BLOCKS)]
    for n, (i, j) in enumerate(todo):
        right = blocks[i, j]
        stage[n] = (dot(poly[i, 0], right) + dot(poly[i, 1], right)).astype(bf16)
        store(stage.at[n], out.at[0, i, :, pl.ds(j * BLOCK, BLOCK)])
    for copy in stores:
        copy.wait()


def update(poly, blocks, norms, grads):
    hbm = pl.BlockSpec(memory_space=pl.ANY)
    vmem = pl.BlockSpec(memory_space=pltpu.VMEM)
    return pl.pallas_call(
        update_kernel,
        out_shape=(
            jax.ShapeDtypeStruct((1, 2, LAT, D), bf16),
            jax.ShapeDtypeStruct((1, 2), f32),
            jax.ShapeDtypeStruct((TOK, D), bf16),
        ),
        in_specs=[vmem] * 4,
        out_specs=(hbm, vmem, hbm),
        scratch_shapes=[
            pltpu.VMEM((2 * BLOCKS - READY, LAT, BLOCK), bf16),
            pltpu.SemaphoreType.DMA((2 * BLOCKS + 1,)),
        ],
        name="update",
        compiler_params=pltpu.CompilerParams(vmem_limit_bytes=30 * 2**20),
    )(*[pltpu.with_memory_space_constraint(a, pltpu.VMEM) for a in (poly, blocks, norms, grads)])


def per_device(saved, top_grad, down_weight, up_weight):
    grads, blocks, poly, norms = backward(
        *[pltpu.with_memory_space_constraint(a, pltpu.HBM) for a in (saved[0], top_grad, down_weight[0], up_weight[0])]
    )
    updates, norm_values, grads = update(poly, blocks, norms, grads)
    return grads[None], updates, norm_values


def solution(mesh):
    return jax.shard_map(
        per_device,
        mesh=mesh,
        in_specs=(
            P("section", "dp", None),
            P("dp", None),
            P("section", None, None),
            P("section", None, None),
        ),
        out_specs=(P("section", "dp", None), P("section", None, None, None), P("section", None)),
        check_vma=False,
    )
```

```python
import math

import jax
import jax.numpy as jnp
from jax import lax
from jax.experimental import pallas as pl
from jax.experimental.pallas import tpu as pltpu
from jax.sharding import PartitionSpec as P

D = 7168
LAT = 256
SECTIONS = 8
ITERS = 5
TOK = 128
ROWS = 16
PAIRS = TOK // ROWS
CHUNKS = 4
WIDE = D // CHUNKS
SMALL = 8
SMALLS = TOK // SMALL
PACK = D // 2
PARTS = ((0, 1280), (1280, 1280), (2560, 1024))
READY = 3
PIECES = ((0, 64), (64, 64), (128, 80), (208, 48))
QUARTERS = len(PIECES)
LAST = QUARTERS - 1
ORDER = (LAST, 0, 1, 2)
HELPED = 2
APART = SECTIONS - HELPED
BLOCKS = 8
BLOCK = D // BLOCKS
PLACES = 8
PEERS = 16
Z = 4

norm_eps = 1e-06
frob_eps = 1e-07
coef_a = 3.4445
coef_b = -4.775
coef_c = 2.0315

MESH = pl.DeviceIdType.MESH
f32 = jnp.float32
bf16 = jnp.bfloat16


def remote(src, dst, send, recv, device):
    return pltpu.make_async_remote_copy(
        src_ref=src, dst_ref=dst, send_sem=send, recv_sem=recv, device_id=device, device_id_type=MESH
    )


def nt_dot(a, b):
    return lax.dot_general(
        a, b, (((1,), (1,)), ((), ())), preferred_element_type=f32
    )


def tn_dot(a, b):
    return lax.dot_general(a, b, (((0,), (0,)), ((), ())), preferred_element_type=f32)


def split(a):
    high = a.astype(bf16)
    return high, (a - high.astype(f32)).astype(bf16)


def dot(a, b):
    return jnp.dot(a, b, preferred_element_type=f32)


def three_dot(a, b):
    (a_high, a_low), (b_high, b_low) = split(a), split(b)
    return dot(a_high, b_high) + (dot(a_high, b_low) + dot(a_low, b_high))


def newton_schulz(gram):
    total = None
    eye = diagonal_mask().astype(f32)
    for step in range(ITERS):
        poly = coef_a * eye + coef_b * gram + coef_c * three_dot(gram, gram)
        if step < ITERS - 1:
            gram = three_dot(three_dot(poly, gram), poly)
        total = poly if total is None else three_dot(poly, total)
    return total


def diagonal_mask():
    return lax.broadcasted_iota(jnp.int32, (LAT, LAT), 0) == lax.broadcasted_iota(
        jnp.int32, (LAT, LAT), 1
    )


def backward_kernel(
    saved, top, w_down, w_up, grads_out, blocks, poly_out, norm_out,
    x_v, x_p, wd_v, wu_v, wut_v, normed_v, og_v, og_p, ig_v, ig_p, inv_v, latent_v, slope_v, act_v, lat_v,
    big_all, small_all, give_v, take_v, relay,
    load_sem, wd_sem, chain_send, chain_recv, big_send, big_recv, small_send, small_recv, store_sem,
    give_send, give_recv, ring_send, ring_recv, core_send, core_recv, poly_send, poly_recv, relay_send, relay_recv,
):
    s = lax.axis_index("section")
    d = lax.axis_index("dp")
    core = lax.rem(d, 2)
    q = lax.div(d, 2)
    x = lax.rem(q, 2)
    z = lax.div(q, 2)
    up = lax.rem(z + 1, Z)
    down = lax.rem(z + 3, Z)
    far = lax.rem(z + 2, Z)
    is_top = s == SECTIONS - 1
    has_lower = s > 0

    def device(z_at, x_at, core_at):
        return (s, z_at * 4 + x_at * 2 + core_at)

    across = device(z, 1 - x, core)
    above = device(up, x, core)
    below = device(down, x, core)
    sibling = device(z, x, 1 - core)

    loads = [
        pltpu.make_async_copy(saved, x_v, load_sem.at[0]),
        pltpu.make_async_copy(w_up, wu_v, load_sem.at[1]),
    ]
    for k in range(BLOCKS):
        part = pl.ds((k % 2) * PACK + (k // 2) * BLOCK, BLOCK)
        loads.append(
            pltpu.make_async_copy(w_down.at[:, pl.ds(k * BLOCK, BLOCK)], wd_v.at[:, part], wd_sem.at[k])
        )
    for load in loads:
        load.start()
    top_load = pltpu.make_async_copy(top, og_v, load_sem.at[2])

    @pl.when(is_top)
    def _():
        top_load.start()

    barrier = pltpu.get_barrier_semaphore()
    for k in range(1, PEERS):
        pl.semaphore_signal(
            barrier, inc=1, device_id=(s, lax.rem(d + k, PEERS)), device_id_type=MESH
        )

    @pl.when(jnp.logical_not(is_top))
    def _():
        pl.semaphore_signal(barrier, inc=1, device_id=(s + 1, d), device_id_type=MESH)

    def pack(flat, packed, i):
        rows = pl.ds(pl.multiple_of(i * ROWS, ROWS), ROWS)
        for k in range(Z):
            even = flat[rows, 2 * k * BLOCK:(2 * k + 1) * BLOCK].astype(f32)
            odd = flat[rows, (2 * k + 1) * BLOCK:(2 * k + 2) * BLOCK].astype(f32)
            cols = slice(k * BLOCK, (k + 1) * BLOCK)
            packed[2 * i, :, cols] = jnp.concatenate([even[:SMALL], odd[:SMALL]], axis=0).astype(bf16)
            packed[2 * i + 1, :, cols] = jnp.concatenate([even[SMALL:], odd[SMALL:]], axis=0).astype(bf16)

    def unpack(packed, flat, i):
        rows = pl.ds(pl.multiple_of(i * ROWS, ROWS), ROWS)
        for k in range(Z):
            cols = slice(k * BLOCK, (k + 1) * BLOCK)
            first = packed[2 * i, :, cols].astype(f32)
            second = packed[2 * i + 1, :, cols].astype(f32)
            even = jnp.concatenate([first[:SMALL], second[:SMALL]], axis=0)
            odd = jnp.concatenate([first[SMALL:], second[SMALL:]], axis=0)
            flat[rows, 2 * k * BLOCK:(2 * k + 1) * BLOCK] = even.astype(bf16)
            flat[rows, (2 * k + 1) * BLOCK:(2 * k + 2) * BLOCK] = odd.astype(bf16)

    helped = s < HELPED
    helper = s >= APART
    partner = (jnp.where(helped, s + APART, jnp.where(helper, s - APART, s)), d)

    @pl.when(jnp.logical_or(helped, helper))
    def _():
        pl.semaphore_signal(barrier, inc=1, device_id=partner, device_id_type=MESH)

    loads[0].wait()

    def norm_rows(m, _):
        rows = pl.ds(pl.multiple_of(m * ROWS, ROWS), ROWS)
        total = jnp.zeros((ROWS, 1), f32)
        for j in range(CHUNKS):
            part = x_v[rows, j * WIDE:(j + 1) * WIDE].astype(f32)
            total += jnp.sum(part * part, axis=1, keepdims=True)
        inv = 1.0 / jnp.sqrt(total * (1.0 / D) + norm_eps)
        inv_v[rows, :] = jnp.broadcast_to(inv, (ROWS, 128))
        for j in range(CHUNKS):
            part = x_v[rows, j * WIDE:(j + 1) * WIDE].astype(f32)
            normed_v[rows, j * WIDE:(j + 1) * WIDE] = (part * inv).astype(bf16)
        return 0

    lax.fori_loop(0, PAIRS, norm_rows, 0)
    loads[1].wait()

    def turn(k, _):
        for odd in range(2):
            cols = pl.ds(pl.multiple_of((2 * k + odd) * BLOCK, BLOCK), BLOCK)
            rows = pl.ds(pl.multiple_of(k * BLOCK, BLOCK), BLOCK)
            wut_v[rows, odd * LAT:(odd + 1) * LAT] = wu_v[:, cols].T
        return 0

    lax.fori_loop(0, Z, turn, 0)
    for load in loads[2:]:
        load.wait()

    def latent_part(k, acc):
        for odd in range(2):
            cols = pl.ds(pl.multiple_of((2 * k + odd) * BLOCK, BLOCK), BLOCK)
            part = pl.ds(pl.multiple_of(odd * PACK + k * BLOCK, BLOCK), BLOCK)
            acc = acc + nt_dot(normed_v[:, cols], wd_v[:, part])
        return acc

    latent = lax.fori_loop(0, Z, latent_part, jnp.zeros((TOK, LAT), f32))
    sigmoid = 1.0 / (1.0 + jnp.exp(-latent))
    latent_v[...] = latent
    act_v[...] = (latent * sigmoid).astype(bf16)
    slope_v[...] = sigmoid * (1.0 + latent * (1.0 - sigmoid))

    both = jnp.logical_and(has_lower, jnp.logical_or(helped, helper))

    @pl.when(both)
    def _():
        pl.semaphore_wait(barrier, PEERS + 1)

    @pl.when(jnp.logical_not(both))
    def _():
        pl.semaphore_wait(barrier, PEERS)

    place = z * 2 + core
    direct = s == 0

    def share_block(src_of, rows, target_core, act, act_own):
        for k in range(Z):
            z_at = lax.rem(z + k, Z)
            for e in range(2):
                half = lax.rem(x + e, 2)
                to_x = jnp.where(direct, half, x)
                slot = jnp.where(direct, x, half)
                src = src_of(pl.ds(pl.multiple_of((z_at * 2 + half) * BLOCK, BLOCK), BLOCK))
                dst = big_all.at[place, slot, rows]
                recv = big_recv.at[place, slot]
                copy = remote(src, dst, big_send, recv, device(z_at, to_x, target_core))
                if k:
                    act(copy)
                else:
                    away = core != target_core
                    if e:
                        away = jnp.logical_or(away, direct)

                    @pl.when(away)
                    def _():
                        act(copy)

                    if act_own is not None:

                        @pl.when(jnp.logical_not(away))
                        def _():
                            act_own(pltpu.make_async_copy(src, dst, recv))

    def share_small(src, rows, target_core, act, act_own):
        slot = jnp.where(direct, x, 0)
        dst = small_all.at[place, slot, rows]
        recv = small_recv.at[place, slot]
        for k in range(Z):
            z_at = lax.rem(z + k, Z)
            copy = remote(src, dst, small_send, recv, device(z_at, x, target_core))
            if k:
                act(copy)
            else:

                @pl.when(core != target_core)
                def _():
                    act(copy)

                if act_own is not None:

                    @pl.when(core == target_core)
                    def _():
                        act_own(pltpu.make_async_copy(src, dst, recv))

        @pl.when(direct)
        def _():
            for k in range(Z):
                z_at = lax.rem(z + k, Z)
                act(remote(src, dst, small_send, recv, device(z_at, 1 - x, target_core)))

    def begin(copy):
        copy.start()

    def left(copy):
        copy.wait_send()

    every = pl.ds(0, TOK)

    def share_normed(act, act_own):
        share_block(lambda cols: normed_v.at[:, cols], every, 0, act, act_own)
        share_small(act_v, every, 1, act, act_own)

    def share_grads(i, act, act_own):
        rows = pl.ds(pl.multiple_of(i * ROWS, ROWS), ROWS)
        share_block(lambda cols: og_v.at[rows, cols], rows, 1, act, act_own)
        share_small(lat_v.at[rows], rows, 0, act, act_own)

    @pl.when(jnp.logical_not(is_top))
    def _():
        share_normed(begin, begin)

    @pl.when(is_top)
    def _():
        top_load.wait()

    def chain_copy(m, j):
        cols = pl.ds(*PARTS[j])
        return remote(
            ig_p.at[m, :, cols], og_p.at[m, :, cols], chain_send.at[m, j], chain_recv.at[m, j],
            (jnp.maximum(s - 1, 0), d),
        )

    def receive(m):
        rows = pl.ds(pl.multiple_of(m * SMALL, SMALL), SMALL)
        acc = jnp.zeros((ROWS, 2 * LAT), f32)
        for j, (at, width) in enumerate(PARTS):

            @pl.when(jnp.logical_not(is_top))
            def _():
                chain_copy(m, j).wait_recv()

            acc += dot(og_p[m, :, at:at + width], wut_v[at:at + width, :])
        act_grad = acc[:SMALL, :LAT] + acc[SMALL:, LAT:]
        lat = (act_grad * slope_v[rows, :]).astype(bf16).astype(f32)
        inv = inv_v[rows, 0:1]
        mean = jnp.sum(lat * latent_v[rows, :], axis=1, keepdims=True) * (1.0 / D)
        pull = inv * inv * mean
        return lat, inv, pull

    def answer(m, lat, inv, pull):
        lat_twice = jnp.concatenate([lat, lat], axis=0).astype(bf16)
        inv_twice = jnp.concatenate([inv, inv], axis=0)
        pull_twice = jnp.concatenate([pull, pull], axis=0)
        for j, (at, width) in enumerate(PARTS):
            cols = slice(at, at + width)
            even = dot(lat_twice, wd_v[:, at:at + width])
            odd = dot(lat_twice, wd_v[:, PACK + at:PACK + at + width])
            ng = jnp.concatenate([even[:SMALL], odd[SMALL:]], axis=0)
            out = og_p[m, :, cols].astype(f32) + inv_twice * ng - pull_twice * x_p[m, :, cols].astype(f32)
            ig_p[m, :, cols] = out.astype(bf16)

            @pl.when(has_lower)
            def _():
                chain_copy(m, j).start()

    def micro(i, _):
        rows = pl.ds(pl.multiple_of(i * ROWS, ROWS), ROWS)
        pack(x_v, x_p, i)

        @pl.when(is_top)
        def _():
            pack(og_v, og_p, i)

        @pl.when(jnp.logical_and(is_top, i == 1))
        def _():
            share_normed(begin, begin)

        first = receive(2 * i)
        answer(2 * i, *first)
        second = receive(2 * i + 1)

        def share_pair():
            lat_v[rows, :] = jnp.concatenate([first[0], second[0]], axis=0).astype(bf16)

            @pl.when(jnp.logical_not(is_top))
            def _():
                unpack(og_p, og_v, i)

            share_grads(i, begin, begin)

        @pl.when(direct)
        def _():
            share_pair()

        answer(2 * i + 1, *second)

        @pl.when(jnp.logical_not(direct))
        def _():
            share_pair()

        unpack(ig_p, ig_v, i)
        return 0

    lax.fori_loop(0, PAIRS, micro, 0)

    store = pltpu.make_async_copy(ig_v, grads_out, store_sem)
    store.start()

    def arrived(p, _):
        for slot in range(2):
            part = big_all.at[p, slot]
            pltpu.make_async_copy(part, part, big_recv.at[p, slot]).wait()
        part = small_all.at[p, 0]
        pltpu.make_async_copy(part, part, small_recv.at[p, 0]).wait()
        return 0

    lax.fori_loop(0, PLACES, arrived, 0)

    @pl.when(direct)
    def _():
        def more(p, _):
            part = small_all.at[p, 1]
            pltpu.make_async_copy(part, part, small_recv.at[p, 1]).wait()
            return 0

        lax.fori_loop(0, PLACES, more, 0)

    ring_copies = []
    alone_copies = []
    core_copies = []

    def quarter_rows(n):
        return pl.ds(*PIECES[n])

    def piece(n):
        return slice(PIECES[n][0], PIECES[n][0] + PIECES[n][1])

    def at(z_at, x_at, n):
        return blocks.at[core, z_at * 2 + x_at, quarter_rows(n)]

    def ring_copy(z_at, x_at, n, to, sem):
        return remote(
            at(z_at, x_at, n), at(z_at, x_at, n), ring_send.at[sem], ring_recv.at[z_at * 2 + x_at, n], to
        )

    def forward(z_at, x_at, n, to):
        copy = ring_copy(z_at, x_at, n, to, 3 * QUARTERS + len(ring_copies) + len(alone_copies))
        if n == LAST:
            alone_copies.append(copy)

            @pl.when(jnp.logical_not(helped))
            def _():
                copy.start()
        else:
            copy.start()
            ring_copies.append(copy)

    def core_copy(z_at, x_at, n):
        return remote(
            at(z_at, x_at, n), at(z_at, x_at, n), core_send, core_recv, sibling
        )

    def to_sibling(z_at, x_at, n):
        copy = core_copy(z_at, x_at, n)
        copy.start()
        core_copies.append(copy)

    def wait(z_at, x_at, n):
        part = at(z_at, x_at, n)
        pltpu.make_async_copy(part, part, ring_recv.at[z_at * 2 + x_at, n]).wait()

    def used(z_at, x_at):
        part = blocks[core, z_at * 2 + x_at]
        return nt_dot(part, part)

    def own_copies(n, act):
        copies = [ring_copy(z, x, n, to, 3 * n + k) for k, to in enumerate((above, below, across))]
        act(core_copy(z, x, n))
        if n != LAST:
            for copy in copies:
                act(copy)
        else:

            @pl.when(jnp.logical_not(helped))
            def _():
                for copy in copies:
                    act(copy)

            @pl.when(helped)
            def _():
                act(remote(at(z, x, n), relay.at[q], relay_send.at[0], relay_recv.at[q], partner))

    @pl.when(direct)
    def _():
        turned = small_all[...].reshape(2 * PLACES * TOK, LAT).T
        right = big_all[...].reshape(2 * PLACES * TOK, BLOCK)
        for n in ORDER:
            blocks[core, q, quarter_rows(n)] = dot(turned[piece(n)], right).astype(bf16)
            own_copies(n, begin)

    def give_copy(n):
        return remote(
            give_v.at[quarter_rows(n)], take_v.at[quarter_rows(n)], give_send.at[n], give_recv.at[n], across
        )

    @pl.when(jnp.logical_not(direct))
    def _():
        turned = small_all[:, 0].reshape(PLACES * TOK, LAT).T
        right = big_all[:, 1 - x].reshape(PLACES * TOK, BLOCK)
        for n in ORDER:
            give_v[quarter_rows(n)] = dot(turned[piece(n)], right).astype(bf16)
            give_copy(n).start()
        mine = dot(turned, big_all[:, x].reshape(PLACES * TOK, BLOCK))
        for n in ORDER:
            give_copy(n).wait_recv()
            total = mine[piece(n)] + take_v[quarter_rows(n)].astype(f32)
            blocks[core, q, quarter_rows(n)] = total.astype(bf16)
            own_copies(n, begin)
        for n in range(QUARTERS):
            give_copy(n).wait_send()

    def near(n):
        wait(down, x, n)
        if n < QUARTERS // 2:
            forward(down, x, n, above)
        to_sibling(down, x, n)
        wait(up, x, n)
        if n >= QUARTERS // 2:
            forward(up, x, n, below)
        to_sibling(up, x, n)
        wait(z, 1 - x, n)
        forward(z, 1 - x, n, above)
        forward(z, 1 - x, n, below)
        to_sibling(z, 1 - x, n)

    def opposite(n):
        wait(far, x, n)
        forward(far, x, n, across)
        to_sibling(far, x, n)

    gram = used(z, x)
    for n in range(LAST):
        near(n)
    for n in (0, 2, 1):
        opposite(n)
    near(LAST)
    opposite(LAST)
    gram += used(down, x)
    gram += used(up, x)
    gram += used(z, 1 - x)
    gram += used(far, x)
    for n in range(QUARTERS):
        for z_at in (up, down):
            wait(z_at, 1 - x, n)
            to_sibling(z_at, 1 - x, n)
    gram += used(up, 1 - x)
    gram += used(down, 1 - x)
    for n in (0, 2, 1, 3):
        wait(far, 1 - x, n)
        to_sibling(far, 1 - x, n)
    gram += used(far, 1 - x)

    squares = jnp.where(diagonal_mask(), gram, 0.0)
    norm = jnp.sqrt(jnp.sum(jnp.sum(squares, axis=1, keepdims=True), axis=0, keepdims=True))
    scale = 1.0 / (norm + frob_eps)
    poly = newton_schulz(gram * scale * scale) * (scale * (0.2 * math.sqrt(D)))
    high, low = split(poly)
    poly_out[core, 0] = high
    poly_out[core, 1] = low
    norm_out[core] = jnp.broadcast_to(norm, (8, 128))
    polys = [
        remote(poly_out.at[core], poly_out.at[core], poly_send.at[0], poly_recv.at[0], sibling),
        remote(norm_out.at[core], norm_out.at[core], poly_send.at[1], poly_recv.at[1], sibling),
    ]
    for copy in polys:
        copy.start()

    for n in range(QUARTERS):
        own_copies(n, left)
    for copy in ring_copies + core_copies:
        copy.wait_send()

    @pl.when(jnp.logical_not(helped))
    def _():
        for copy in alone_copies:
            copy.wait_send()

    def finish(j, _):
        right = blocks[core, j]
        blocks[core, j] = (dot(high, right) + dot(low, right)).astype(bf16)
        return 0

    lax.fori_loop(0, READY, finish, 0)
    theirs = 1 - core
    pltpu.make_async_copy(blocks.at[theirs], blocks.at[theirs], core_recv).wait()
    pltpu.make_async_copy(poly_out.at[theirs], poly_out.at[theirs], poly_recv.at[0]).wait()
    pltpu.make_async_copy(norm_out.at[theirs], norm_out.at[theirs], poly_recv.at[1]).wait()

    @pl.when(helper)
    def _():
        relays = []

        def pass_to(z_at, x_at, to):
            n = z_at * 2 + x_at
            copy = remote(relay.at[n], relay.at[n], relay_send.at[len(relays)], relay_recv.at[n], to)
            copy.start()
            relays.append(copy)

        def arrive(z_at, x_at):
            n = z_at * 2 + x_at
            pltpu.make_async_copy(relay.at[n], relay.at[n], relay_recv.at[n]).wait()

        def deliver(z_at, x_at):
            n = z_at * 2 + x_at
            copy = remote(
                relay.at[n], blocks.at[core, n, quarter_rows(LAST)],
                relay_send.at[len(relays)], ring_recv.at[n, LAST], partner,
            )
            copy.start()
            relays.append(copy)

        arrive(z, x)
        pass_to(z, x, above)
        pass_to(z, x, below)
        pass_to(z, x, across)
        arrive(down, x)
        pass_to(down, x, above)
        deliver(down, x)
        arrive(up, x)
        deliver(up, x)
        arrive(z, 1 - x)
        pass_to(z, 1 - x, above)
        pass_to(z, 1 - x, below)
        deliver(z, 1 - x)
        arrive(far, x)
        pass_to(far, x, across)
        deliver(far, x)
        for z_at in (up, down, far):
            arrive(z_at, 1 - x)
            deliver(z_at, 1 - x)
        for copy in relays:
            copy.wait_send()

    share_normed(left, None)

    def sent(m, _):
        share_grads(m, left, None)

        @pl.when(has_lower)
        def _():
            for j in range(len(PARTS)):
                chain_copy(2 * m, j).wait_send()
                chain_copy(2 * m + 1, j).wait_send()

        return 0

    lax.fori_loop(0, PAIRS, sent, 0)
    for copy in polys:
        copy.wait_send()
    store.wait()


def backward(saved, top, w_down, w_up):
    hbm = pl.BlockSpec(memory_space=pl.ANY)
    vmem = pl.BlockSpec(memory_space=pltpu.VMEM)
    dma = pltpu.SemaphoreType.DMA
    return pl.pallas_call(
        backward_kernel,
        out_shape=(
            pltpu.VMEM((TOK, D), bf16),
            pltpu.VMEM((2, BLOCKS, LAT, BLOCK), bf16),
            pltpu.VMEM((2, 2, LAT, LAT), bf16),
            pltpu.VMEM((2, 8, 128), f32),
        ),
        in_specs=[hbm] * 4,
        out_specs=(hbm, vmem, vmem, vmem),
        scratch_shapes=[
            pltpu.VMEM((TOK, D), bf16),
            pltpu.VMEM((SMALLS, ROWS, PACK), bf16),
            pltpu.VMEM((LAT, D), bf16),
            pltpu.VMEM((LAT, D), bf16),
            pltpu.VMEM((PACK, 2 * LAT), bf16),
            pltpu.VMEM((TOK, D), bf16),
            pltpu.VMEM((TOK, D), bf16),
            pltpu.VMEM((SMALLS, ROWS, PACK), bf16),
            pltpu.VMEM((TOK, D), bf16),
            pltpu.VMEM((SMALLS, ROWS, PACK), bf16),
            pltpu.VMEM((TOK, 128), f32),
            pltpu.VMEM((TOK, LAT), f32),
            pltpu.VMEM((TOK, LAT), f32),
            pltpu.VMEM((TOK, LAT), bf16),
            pltpu.VMEM((TOK, LAT), bf16),
            pltpu.VMEM((PLACES, 2, TOK, BLOCK), bf16),
            pltpu.VMEM((PLACES, 2, TOK, LAT), bf16),
            pltpu.VMEM((LAT, BLOCK), bf16),
            pltpu.VMEM((LAT, BLOCK), bf16),
            pltpu.VMEM((BLOCKS, PIECES[LAST][1], BLOCK), bf16),
            dma((3,)),
            dma((BLOCKS,)),
            dma((SMALLS, len(PARTS))),
            dma((SMALLS, len(PARTS))),
            dma(()),
            dma((PLACES, 2)),
            dma(()),
            dma((PLACES, 2)),
            dma(()),
            dma((QUARTERS,)),
            dma((QUARTERS,)),
            dma((7 * QUARTERS,)),
            dma((BLOCKS, QUARTERS)),
            dma(()),
            dma(()),
            dma((2,)),
            dma((2,)),
            dma((14,)),
            dma((BLOCKS,)),
        ],
        name="backward",
        compiler_params=pltpu.CompilerParams(
            collective_id=0, has_side_effects=True, vmem_limit_bytes=40 * 2**20
        ),
    )(saved, top, w_down, w_up)


def update_kernel(poly, blocks, norms, grads, out, norm_out, grads_out, stage, store_sem):
    mine = lax.rem(lax.axis_index("dp"), 2)
    theirs = 1 - mine
    stores = []

    def store(src, dst):
        copy = pltpu.make_async_copy(src, dst, store_sem.at[len(stores)])
        copy.start()
        stores.append(copy)

    for j in range(READY):
        store(blocks.at[mine, j], out.at[0, mine, :, pl.ds(j * BLOCK, BLOCK)])
    store(grads, grads_out)
    column = lax.broadcasted_iota(jnp.int32, (1, 2), 1)
    norm_out[...] = jnp.where(column == 0, norms[0, 0:1, 0:1], norms[1, 0:1, 0:1])
    todo = [(mine, j) for j in range(READY, BLOCKS)] + [(theirs, j) for j in range(BLOCKS)]
    for n, (i, j) in enumerate(todo):
        right = blocks[i, j]
        stage[n] = (dot(poly[i, 0], right) + dot(poly[i, 1], right)).astype(bf16)
        store(stage.at[n], out.at[0, i, :, pl.ds(j * BLOCK, BLOCK)])
    for copy in stores:
        copy.wait()


def update(poly, blocks, norms, grads):
    hbm = pl.BlockSpec(memory_space=pl.ANY)
    vmem = pl.BlockSpec(memory_space=pltpu.VMEM)
    return pl.pallas_call(
        update_kernel,
        out_shape=(
            jax.ShapeDtypeStruct((1, 2, LAT, D), bf16),
            jax.ShapeDtypeStruct((1, 2), f32),
            jax.ShapeDtypeStruct((TOK, D), bf16),
        ),
        in_specs=[vmem] * 4,
        out_specs=(hbm, vmem, hbm),
        scratch_shapes=[
            pltpu.VMEM((2 * BLOCKS - READY, LAT, BLOCK), bf16),
            pltpu.SemaphoreType.DMA((2 * BLOCKS + 1,)),
        ],
        name="update",
        compiler_params=pltpu.CompilerParams(vmem_limit_bytes=30 * 2**20),
    )(*[pltpu.with_memory_space_constraint(a, pltpu.VMEM) for a in (poly, blocks, norms, grads)])


def per_device(saved, top_grad, down_weight, up_weight):
    grads, blocks, poly, norms = backward(
        *[pltpu.with_memory_space_constraint(a, pltpu.HBM) for a in (saved[0], top_grad, down_weight[0], up_weight[0])]
    )
    updates, norm_values, grads = update(poly, blocks, norms, grads)
    return grads[None], updates, norm_values


def solution(mesh):
    return jax.shard_map(
        per_device,
        mesh=mesh,
        in_specs=(
            P("section", "dp", None),
            P("dp", None),
            P("section", None, None),
            P("section", None, None),
        ),
        out_specs=(P("section", "dp", None), P("section", None, None, None), P("section", None)),
        check_vma=False,
    )
```
